128 devices in a mesh: dp: 4 (over y), ctx: 32 (over z, x, core).
Axes of the slice: x: 4, y: 4, z: 4, core: 2. Of those that a mesh axis runs over, the one named last changes fastest.
Arguments:
- hidden_in: bfloat16 [4, 4096, 1024], P('dp', 'ctx'), may hold values from -6 to 6
- positions: int32 [4, 4096], P('dp', 'ctx'), may hold values from 0 to 8190, as said below
- block_of: int32 [64], replicated, may hold values from 0 to 63, as said below
- attn_gain: bfloat16 [1024], P('dp'), may hold values from 0.099609375 to 1.8984375
- query_weight: bfloat16 [1024, 1024], P('dp'), may hold values from -0.1875 to 0.1875
- key_weight: bfloat16 [1024, 512], P('dp'), may hold values from -0.1875 to 0.1875
- value_weight: bfloat16 [1024, 512], P('dp'), may hold values from -0.1875 to 0.1875
- out_weight: bfloat16 [1024, 1024], P('dp'), may hold values from -2 to 2
- query_gain: bfloat16 [64], P('dp'), may hold values from 0.099609375 to 1.8984375
- key_gain: bfloat16 [64], P('dp'), may hold values from 0.099609375 to 1.8984375
- ffn_gain: bfloat16 [1024], P('dp'), may hold values from 0.099609375 to 1.8984375
- gate_weight: bfloat16 [1024, 4608], P('dp'), may hold values from -0.1875 to 0.1875
- up_weight: bfloat16 [1024, 4608], P('dp'), may hold values from -0.1875 to 0.1875
- down_weight: bfloat16 [4608, 1024], P('dp'), may hold values from -0.09375 to 0.09375
- cotangent: bfloat16 [4, 4096, 1024], P('dp', 'ctx'), may hold values from -6 to 6
Outputs:
- layer_out: bfloat16 [4, 4096, 1024], P('dp', 'ctx')
- input_grad: bfloat16 [4, 4096, 1024], P('dp', 'ctx')
- attn_gain_grad: float32 [1024], P('dp')
- query_weight_grad: float32 [1024, 1024], P('dp')
- key_weight_grad: float32 [1024, 512], P('dp')
- value_weight_grad: float32 [1024, 512], P('dp')
- out_weight_grad: float32 [1024, 1024], P('dp')
- query_gain_grad: float32 [64], P('dp')
- key_gain_grad: float32 [64], P('dp')
- ffn_gain_grad: float32 [1024], P('dp')
- gate_weight_grad: float32 [1024, 4608], P('dp')
- up_weight_grad: float32 [1024, 4608], P('dp')
- down_weight_grad: float32 [4608, 1024], P('dp')
The draws below stay inside these ranges and needn't reach their ends.
Inputs may be any that keep to these rules, and one draw needn't show every extreme that they name: `block_of`: entries 2c and 2c + 1 (the slots of ctx index c) are a block b of the sequence's first half and its mirror, the block that counts back by b from the last; every block once. Each sequence's positions are an offset of the sequence below 4096 plus the row's causal order.
All inputs are finite; a program needn't handle non-finite values.
Results may differ from the reference program's by a relative error of at most 0.025.
Values may be sent and summed in bfloat16 or wider, within the bound.
A program may use at most 192 MiB of HBM per device.

```python
import jax
import jax.numpy as jnp
from jax import lax

D = 1024
HEADS = 16
KVH = 8
HD = 64
FF = 4608
BLK = 64
SEQ_LEN = 4096
SEQS = 4
N_CTX = 32


def early_blocks(key):
    return jax.random.permutation(key, N_CTX).astype(jnp.int32)


def pair_table(early_ids):
    late_ids = 2 * N_CTX - 1 - early_ids
    return jnp.stack([early_ids, late_ids], axis=1).reshape(2 * N_CTX).astype(jnp.int32)


def draw_block_of(key, part):
    early_ids = early_blocks(key)
    return pair_table(early_ids)


def draw_positions(key, part):
    early_ids = early_blocks(key)
    key = jax.random.fold_in(key, 23)
    slot_table = pair_table(early_ids)
    in_block = jnp.arange(BLK, dtype=jnp.int32)
    causal_order = (slot_table[:, None] * BLK + in_block[None, :]).reshape(SEQ_LEN)
    offsets = jax.random.randint(key, (SEQS, 1), 0, SEQ_LEN, dtype=jnp.int32)
    return (offsets + causal_order[None, :]).astype(jnp.int32)


def levels(rng, extent, pieces, least, largest):
    def one(axis_at, parts):
        steps = jax.random.uniform(jax.random.fold_in(jax.random.fold_in(rng, 6), axis_at), (parts,), jnp.float32, least / len(pieces), largest / len(pieces))
        return jnp.repeat(jnp.exp(steps), extent[axis_at] // parts).reshape((-1,) + (1,) * (len(extent) - axis_at - 1))

    loudness = one(*pieces[0])
    for cut in pieces[1:]:
        loudness = loudness * one(*cut)
    return loudness


def scatter_about(rng, dims, scale, bound, cuts=(), kind=jnp.bfloat16):
    drawn = scale * jax.random.normal(rng, dims, jnp.float32)
    if cuts:
        drawn = drawn * levels(rng, dims, cuts, -0.22, 0.18)
    return jnp.clip(drawn, -bound, bound).astype(kind)


def setup_inputs(seed: int = 0) -> dict:
    key_list = jax.random.split(jax.random.key(seed), 16)
    return {
        "hidden_in": scatter_about(key_list[0], (SEQS, SEQ_LEN, D), 1.0, 6.0, ((0, 4), (1, 32))),
        "positions": draw_positions(jax.random.fold_in(key_list[15], 71), 0),
        "block_of": draw_block_of(jax.random.fold_in(key_list[15], 71), 0),
        "attn_gain": jnp.clip(1.0 + 0.18 * jax.random.normal(key_list[3], (D,), jnp.float32), 0.099609375, 1.8984375).astype(jnp.bfloat16),
        "query_weight": scatter_about(key_list[4], (D, HEADS * HD), D ** -0.5, 0.1875, ((0, 4),)),
        "key_weight": scatter_about(key_list[5], (D, KVH * HD), D ** -0.5, 0.1875, ((0, 4),)),
        "value_weight": scatter_about(key_list[6], (D, KVH * HD), D ** -0.5, 0.1875, ((0, 4),)),
        "out_weight": scatter_about(key_list[7], (HEADS * HD, D), (max(D // 128, 1)) ** -0.5, 2.0, ((0, 4),)),
        "query_gain": jnp.clip(1.0 + 0.18 * jax.random.normal(key_list[8], (HD,), jnp.float32), 0.099609375, 1.8984375).astype(jnp.bfloat16),
        "key_gain": jnp.clip(1.0 + 0.18 * jax.random.normal(key_list[9], (HD,), jnp.float32), 0.099609375, 1.8984375).astype(jnp.bfloat16),
        "ffn_gain": jnp.clip(1.0 + 0.18 * jax.random.normal(key_list[10], (D,), jnp.float32), 0.099609375, 1.8984375).astype(jnp.bfloat16),
        "gate_weight": scatter_about(key_list[11], (D, FF), D ** -0.5, 0.1875, ((0, 4),)),
        "up_weight": scatter_about(key_list[12], (D, FF), D ** -0.5, 0.1875, ((0, 4),)),
        "down_weight": scatter_about(key_list[13], (FF, D), FF ** -0.5, 0.09375, ((0, 4),)),
        "cotangent": scatter_about(key_list[14], (SEQS, SEQ_LEN, D), 1.0, 6.0, ((0, 4), (1, 32))),
    }


NORM_EPS = 1e-05
ROPE_BASE = 1000000.0
MASKED_SCORE = -1e+30

@jax.custom_vjp
def low(v):
    return lax.optimization_barrier(v.astype(jnp.bfloat16)).astype(jnp.float32)

@jax.custom_vjp
def low_back(v):
    return v

def low_keep(v):
    return (low(v), None)

def low_pass(kept, grad):
    return (grad,)

def back_keep(v):
    return (v, None)

def back_low(kept, grad):
    return (low(grad),)
low.defvjp(low_keep, low_pass)
low_back.defvjp(back_keep, back_low)

def matmul(left, right):
    return jnp.dot(left, right, precision=lax.Precision.HIGHEST)

def rms_scale(values, gain):
    return values * lax.rsqrt(lax.optimization_barrier(jnp.mean(values * values, axis=-1, keepdims=True)) + NORM_EPS) * gain

def rope_tables(places):
    half_dim = HD // 2
    frequency = ROPE_BASE ** (-2.0 * jnp.arange(half_dim, dtype=jnp.float32) / HD)
    angles = places.astype(jnp.float32)[:, None] * frequency[None, :]
    return (jnp.cos(angles), jnp.sin(angles))

def rotate(values, cosine, sine_table):
    half_dim = HD // 2
    front_half = values[..., :half_dim]
    back_half = values[..., half_dim:]
    cos_rows = cosine[:, None, :]
    sin_rows = sine_table[:, None, :]
    return jnp.concatenate([front_half * cos_rows - back_half * sin_rows, back_half * cos_rows + front_half * sin_rows], axis=-1)

def qk_post(cosine, sine_table, query_flat, key_flat, gain_q, gain_k):
    row_count = query_flat.shape[0]
    query_heads = rotate(rms_scale(query_flat.reshape(row_count, HEADS, HD), gain_q), cosine, sine_table)
    key_heads = rotate(rms_scale(key_flat.reshape(row_count, KVH, HD), gain_k), cosine, sine_table)
    return (query_heads.reshape(row_count, HEADS * HD), key_heads.reshape(row_count, KVH * HD))

def swiglu(gate_proj, upward):
    return jax.nn.silu(gate_proj) * upward

def attend(queries, keys_rot, values_low, causal_order):
    block_rows = min(512, SEQ_LEN)
    block_count = SEQ_LEN // block_rows
    group_size = HEADS // KVH
    score_scale = HD ** (-0.5)
    key_heads = keys_rot.reshape(SEQ_LEN, KVH, HD)
    value_heads = values_low.reshape(SEQ_LEN, KVH, HD)

    def one_block(block_args):
        query_block, order_block = block_args
        query_heads = query_block.reshape(block_rows, KVH, group_size, HD)
        scores = jnp.einsum('qkgd,skd->qkgs', query_heads, key_heads, precision=lax.Precision.HIGHEST) * score_scale
        scores = low_back(scores)
        allowed = causal_order[None, None, None, :] <= order_block[:, None, None, None]
        attn_probs = jax.nn.softmax(jnp.where(allowed, scores, MASKED_SCORE), axis=-1)
        mixed_out = jnp.einsum('qkgs,skd->qkgd', low(attn_probs), value_heads, precision=lax.Precision.HIGHEST)
        return mixed_out.reshape(block_rows, HEADS * HD)
    blocks = lax.map(jax.checkpoint(one_block), (queries.reshape(block_count, block_rows, HEADS * HD), causal_order.reshape(block_count, block_rows)))
    return blocks.reshape(SEQ_LEN, HEADS * HD)

def layer(params, hidden, places, causal_order):
    attn_gain, query_weight, key_weight, value_weight, out_weight, query_gain, key_gain, ffn_gain, gate_weight, up_weight, down_weight = params
    cosine, sine_table = rope_tables(places)
    attn_in = low(rms_scale(hidden, attn_gain))
    query_raw = low_back(matmul(attn_in, query_weight))
    key_raw = low_back(matmul(attn_in, key_weight))
    value_raw = low_back(matmul(attn_in, value_weight))
    query_rot, key_rot = qk_post(cosine, sine_table, query_raw, key_raw, query_gain, key_gain)
    mixed_out = attend(low(query_rot), low(key_rot), low(value_raw), causal_order)
    attn_low = low(low_back(mixed_out))
    after_attn = hidden + low_back(matmul(attn_low, out_weight))
    ffn_in = low(rms_scale(after_attn, ffn_gain))
    gate_proj = low_back(matmul(ffn_in, gate_weight))
    up_proj = low_back(matmul(ffn_in, up_weight))
    activated = low(swiglu(gate_proj, up_proj))
    return after_attn + low_back(matmul(activated, down_weight))

def reference(hidden_in, positions, block_of, attn_gain, query_weight, key_weight, value_weight, out_weight, query_gain, key_gain, ffn_gain, gate_weight, up_weight, down_weight, cotangent):
    in_block = jnp.arange(BLK, dtype=jnp.int32)
    causal_order = (block_of[:, None] * BLK + in_block[None, :]).reshape(SEQ_LEN).astype(jnp.int32)
    params = (attn_gain.astype(jnp.float32), query_weight.astype(jnp.float32), key_weight.astype(jnp.float32), value_weight.astype(jnp.float32), out_weight.astype(jnp.float32), query_gain.astype(jnp.float32), key_gain.astype(jnp.float32), ffn_gain.astype(jnp.float32), gate_weight.astype(jnp.float32), up_weight.astype(jnp.float32), down_weight.astype(jnp.float32))

    def forward(weights, hidden):

        def one_sequence(seq_pair):
            return layer(weights, seq_pair[0], seq_pair[1], causal_order)
        return lax.map(one_sequence, (hidden, positions))
    result, pullback = jax.vjp(forward, params, hidden_in.astype(jnp.float32))
    weight_grads, hidden_grad = pullback(cotangent.astype(jnp.float32))
    return (result.astype(jnp.bfloat16), hidden_grad.astype(jnp.bfloat16), weight_grads[0], weight_grads[1], weight_grads[2], weight_grads[3], weight_grads[4], weight_grads[5], weight_grads[6], weight_grads[7], weight_grads[8], weight_grads[9], weight_grads[10])
```

```python
import jax
import jax.numpy as jnp
import numpy as np
from jax import lax
from jax.experimental import pallas as pl
from jax.experimental.pallas import tpu as pltpu
from jax.sharding import Mesh, PartitionSpec as P

HEADS = 16
KVH = 8
HD = 64
BLK = 64
LINE = 8
QUARTERS = 4
HALF = 512
ROWS = 1024

NORM_EPS = 1e-05
ROPE_BASE = 1000000.0
EXP2_SCALE = float(HD ** -0.5 * np.log2(np.e))
SCORE_SCALE = HD ** -0.5

F32 = jnp.float32
BF16 = jnp.bfloat16


def dot(left, right, left_dim=1, right_dim=0):
    return lax.dot_general(
        left, right, (((left_dim,), (right_dim,)), ((), ())), preferred_element_type=F32
    )


def rms_scale(values, gain):
    return values * lax.rsqrt(jnp.mean(values * values, axis=-1, keepdims=True) + NORM_EPS) * gain


def head_norm_rope(raw, gain, cosine, sine):
    scaled = (
        raw
        * lax.rsqrt(jnp.mean(raw * raw, axis=1, keepdims=True) + NORM_EPS)
        * gain[None, :, None]
    )
    front = scaled[:, : HD // 2]
    back = scaled[:, HD // 2 :]
    return jnp.concatenate(
        [front * cosine - back * sine, back * cosine + front * sine], axis=1
    )


def scores_of(keys_t, queries_t):
    return dot(keys_t, queries_t, 0, 0)


def attend_kernel(q_ref, kv_ref, qo_ref, ko_ref, mixed_ref, low_ref, log_ref):
    for half in range(2):
        cols = slice(half * HALF, (half + 1) * HALF)
        q_order = qo_ref[:, cols]
        for head in range(2):
            q_t = q_ref[head * HD : (head + 1) * HD, cols]

            def quarter(z, carried):
                acc, total = carried
                for k_half in range(half + 1):
                    keys = slice(k_half * HALF, (k_half + 1) * HALF)
                    probs = jnp.exp2(scores_of(kv_ref[z, 0:HD, keys], q_t) * EXP2_SCALE)
                    if k_half == half:
                        allowed = ko_ref[z, keys, :] <= q_order
                        probs = jnp.where(allowed, probs, 0.0)
                    total = total + jnp.sum(probs, axis=0, keepdims=True)
                    acc = acc + dot(kv_ref[z, HD : 2 * HD, keys], probs.astype(BF16))
                return acc, total

            acc, total = lax.fori_loop(
                0,
                QUARTERS,
                quarter,
                (jnp.zeros((HD, HALF), F32), jnp.zeros((1, HALF), F32)),
            )
            mixed = acc / total
            mixed_ref[head * HD : (head + 1) * HD, cols] = mixed
            low_ref[head * HD : (head + 1) * HD, cols] = mixed.astype(BF16)
            log_ref[head : head + 1, cols] = jnp.log2(total)


def attend(q_t, kv_t, q_order, k_order):
    return pl.pallas_call(
        attend_kernel,
        out_shape=(
            jax.ShapeDtypeStruct((2 * HD, ROWS), F32),
            jax.ShapeDtypeStruct((2 * HD, ROWS), BF16),
            jax.ShapeDtypeStruct((2, ROWS), F32),
        ),
        in_specs=[pl.BlockSpec(memory_space=pltpu.VMEM)] * 4,
        out_specs=(pl.BlockSpec(memory_space=pltpu.VMEM),) * 3,
        compiler_params=pltpu.CompilerParams(vmem_limit_bytes=40 * 2**20),
        cost_estimate=pl.CostEstimate(flops=2 * 10**9, bytes_accessed=4 * 10**6, transcendentals=6 * 10**6),
    )(q_t, kv_t, q_order, k_order)


def attend_back_kernel(
    q_ref, kv_ref, qo_ref, ko_ref, mixed_ref, log_ref, grad_ref, dq_ref, dkv_ref, dkv_acc
):
    dkv_acc[...] = jnp.zeros_like(dkv_acc)
    for half in range(2):
        cols = slice(half * HALF, (half + 1) * HALF)
        q_order = qo_ref[:, cols]
        for head in range(2):
            rows = slice(head * HD, (head + 1) * HD)
            q_t = q_ref[rows, cols]
            grad_t = grad_ref[rows, cols]
            log_total = log_ref[head : head + 1, cols]
            prob_dot = jnp.sum(
                mixed_ref[rows, cols] * grad_t.astype(F32), axis=0, keepdims=True
            )

            def quarter(z, dq):
                for k_half in range(half + 1):
                    keys = slice(k_half * HALF, (k_half + 1) * HALF)
                    k_t = kv_ref[z, 0:HD, keys]
                    v_t = kv_ref[z, HD : 2 * HD, keys]
                    probs = jnp.exp2(scores_of(k_t, q_t) * EXP2_SCALE - log_total)
                    if k_half == half:
                        allowed = ko_ref[z, keys, :] <= q_order
                        probs = jnp.where(allowed, probs, 0.0)
                    dkv_acc[z, HD : 2 * HD, keys] += dot(grad_t, probs.astype(BF16), 1, 1)
                    score_grad = (probs * (scores_of(v_t, grad_t) - prob_dot)).astype(BF16)
                    dkv_acc[z, 0:HD, keys] += dot(q_t, score_grad, 1, 1)
                    dq = dq + dot(k_t, score_grad)
                return dq

            dq = lax.fori_loop(0, QUARTERS, quarter, jnp.zeros((HD, HALF), F32))
            dq_ref[rows, cols] = dq * SCORE_SCALE
    for z in range(QUARTERS):
        dkv_ref[z, 0:HD, :] = (dkv_acc[z, 0:HD, :] * SCORE_SCALE).astype(BF16)
        dkv_ref[z, HD : 2 * HD, :] = dkv_acc[z, HD : 2 * HD, :].astype(BF16)


def attend_back(q_t, kv_t, q_order, k_order, mixed, log_total, mixed_grad):
    return pl.pallas_call(
        attend_back_kernel,
        out_shape=(
            jax.ShapeDtypeStruct((2 * HD, ROWS), F32),
            jax.ShapeDtypeStruct((QUARTERS, 2 * HD, ROWS), BF16),
        ),
        in_specs=[pl.BlockSpec(memory_space=pltpu.VMEM)] * 7,
        out_specs=(pl.BlockSpec(memory_space=pltpu.VMEM),) * 2,
        scratch_shapes=[pltpu.VMEM((QUARTERS, 2 * HD, ROWS), F32)],
        compiler_params=pltpu.CompilerParams(vmem_limit_bytes=40 * 2**20),
        cost_estimate=pl.CostEstimate(flops=4 * 10**9, bytes_accessed=6 * 10**6, transcendentals=6 * 10**6),
    )(q_t, kv_t, q_order, k_order, mixed, log_total, mixed_grad)


LINE_AXES = ("x", "core")


def line_gather(rows):
    width = rows.shape[1]
    parts = lax.all_gather(rows.reshape(2, BLK, width), LINE_AXES, axis=1)
    return parts.reshape(ROWS, width)


def line_scatter(partial):
    width = partial.shape[1]
    parts = partial.reshape(2, LINE, BLK, width).transpose(1, 0, 2, 3)
    return lax.psum_scatter(
        parts.reshape(LINE * 2 * BLK, width), LINE_AXES, scatter_dimension=0, tiled=True
    )


SWAP = [(a * 4 + b, b * 4 + a) for a in range(4) for b in range(4)]


def on_device(
    hidden_in,
    positions,
    block_of,
    attn_gain,
    query_weight,
    key_weight,
    value_weight,
    out_weight,
    query_gain,
    key_gain,
    ffn_gain,
    gate_weight,
    up_weight,
    down_weight,
    cotangent,
):
    z_at = lax.axis_index("z")
    x_at = lax.axis_index("x")
    core_at = lax.axis_index("core")
    place = x_at * 2 + core_at
    dp_at = lax.axis_index("dp")

    hidden_rows = hidden_in[0]
    grad_rows = cotangent[0]

    in_block = jnp.arange(BLK, dtype=jnp.int32)
    blocks = block_of.reshape(QUARTERS, LINE, 2).transpose(0, 2, 1)
    order_all = (blocks[..., None] * BLK + in_block).reshape(QUARTERS, ROWS)
    own_order = lax.dynamic_index_in_dim(order_all, z_at, 0, keepdims=True)
    k_order = order_all.reshape(QUARTERS, ROWS, 1)
    first_block = lax.dynamic_index_in_dim(block_of, 2 * (z_at * LINE + place), 0, keepdims=False)
    offset = positions[0, 0] - first_block * BLK
    frequency = ROPE_BASE ** (-2.0 * jnp.arange(HD // 2, dtype=F32) / HD)
    angles = (own_order + offset).astype(F32) * frequency[:, None]
    cosine, sine = jnp.cos(angles), jnp.sin(angles)

    gains = lax.all_gather(
        jnp.concatenate([attn_gain, ffn_gain, query_gain, key_gain]), "dp", axis=0
    ).astype(F32)
    attn_gain_all = gains[:, 0:256].reshape(1024)
    ffn_gain_all = gains[:, 256:512].reshape(1024)
    query_gain_all = gains[:, 512:528].reshape(HD)
    key_gain_all = gains[:, 528:544].reshape(HD)
    qkv_own = jnp.concatenate(
        [
            lax.dynamic_slice_in_dim(query_weight, place * 128, 128, axis=1),
            lax.dynamic_slice_in_dim(key_weight, place * 64, 64, axis=1),
            lax.dynamic_slice_in_dim(value_weight, place * 64, 64, axis=1),
        ],
        axis=1,
    )
    qkv_weight = lax.all_gather(qkv_own, "dp", axis=0, tiled=True)
    out_own = lax.dynamic_slice_in_dim(out_weight, core_at * 128 + x_at * 32, 32, axis=0)
    out_slice = lax.all_gather(
        lax.ppermute(out_own, ("dp", "x"), SWAP), "dp", axis=0, tiled=True
    )

    def ff_columns(weight):
        parts = weight.reshape(256, 4, LINE, 144)
        return lax.dynamic_slice_in_dim(parts, place, 1, axis=2).reshape(256, 576)

    gate_up = lax.all_gather(
        jnp.concatenate([ff_columns(gate_weight), ff_columns(up_weight)], axis=1),
        "dp",
        axis=0,
        tiled=True,
    )
    down_slice = lax.all_gather(
        lax.dynamic_slice_in_dim(down_weight, place * 144, 144, axis=0), "dp", axis=0, tiled=True
    )

    hidden = hidden_rows.astype(F32)
    line_hidden = line_gather(hidden_rows)
    attn_in = rms_scale(line_hidden.astype(F32), attn_gain_all).astype(BF16)
    qkv_t = dot(qkv_weight, attn_in, 0, 1)
    q_rot, q_back = jax.vjp(
        lambda r, g: head_norm_rope(r, g, cosine, sine),
        qkv_t[0:128].reshape(2, HD, ROWS),
        query_gain_all,
    )
    k_rot, k_back = jax.vjp(
        lambda r, g: head_norm_rope(r, g, cosine, sine),
        qkv_t[128:192].reshape(1, HD, ROWS),
        key_gain_all,
    )
    q_low = q_rot.reshape(128, ROWS).astype(BF16)
    kv_low = jnp.concatenate([k_rot.reshape(HD, ROWS), qkv_t[192:256]], axis=0).astype(BF16)
    kv_all = lax.all_gather(kv_low, "z", axis=0)
    mixed, attn_low, log_total = attend(q_low, kv_all, own_order, k_order)
    after_attn = hidden + line_scatter(dot(attn_low, out_slice, 0, 0).astype(BF16)).astype(F32)
    normed_ffn, norm_ffn_back = jax.vjp(rms_scale, after_attn, ffn_gain_all)
    ffn_in = line_gather(normed_ffn.astype(BF16))
    gate_up_proj = dot(ffn_in, gate_up)
    gate_proj = gate_up_proj[:, :576]
    up_proj = gate_up_proj[:, 576:]
    activated, swiglu_back = jax.vjp(lambda g, u: jax.nn.silu(g) * u, gate_proj, up_proj)
    activated_low = activated.astype(BF16)
    layer_out = (
        after_attn + line_scatter(dot(activated_low, down_slice).astype(BF16)).astype(F32)
    ).astype(BF16)

    residual_grad = grad_rows.astype(F32)
    branch_low = line_gather(grad_rows)
    activated_grad = dot(branch_low, down_slice, 1, 1)
    gate_grad, up_grad = swiglu_back(activated_grad)
    gate_up_grad = jnp.concatenate([gate_grad, up_grad], axis=1).astype(BF16)
    ffn_in_grad = line_scatter(dot(gate_up_grad, gate_up, 1, 1).astype(BF16)).astype(F32)
    mid_part, ffn_gain_part = norm_ffn_back(ffn_in_grad)
    mid_grad = residual_grad + mid_part
    branch_attn = line_gather(mid_grad.astype(BF16))
    mixed_grad = dot(out_slice, branch_attn, 1, 1).astype(BF16)
    q_grad, kv_grad_all = attend_back(
        q_low, kv_all, own_order, k_order, mixed, log_total, mixed_grad
    )
    kv_grad = lax.psum_scatter(kv_grad_all, "z", scatter_dimension=0, tiled=False).astype(F32)
    q_pre, q_gain_part = q_back(q_grad.reshape(2, HD, ROWS))
    k_pre, k_gain_part = k_back(kv_grad[0:HD].reshape(1, HD, ROWS))
    qkv_pre = jnp.concatenate(
        [q_pre.reshape(128, ROWS), k_pre.reshape(HD, ROWS), kv_grad[HD:]], axis=0
    ).astype(BF16)
    attn_in_grad = line_scatter(dot(qkv_pre, qkv_weight, 0, 1).astype(BF16)).astype(F32)
    unused, norm_attn_back = jax.vjp(rms_scale, hidden, attn_gain_all)
    hidden_part, attn_gain_part = norm_attn_back(attn_in_grad)
    input_grad = (mid_grad + hidden_part).astype(BF16)

    gain_sums = lax.psum(
        jnp.concatenate([attn_gain_part, ffn_gain_part, q_gain_part, k_gain_part]),
        ("dp", "z", "x", "core"),
    )

    def own_slice(begin, size):
        return lax.dynamic_slice_in_dim(gain_sums[begin : begin + size], dp_at * (size // 4), size // 4)

    def reduce_rows(part):
        rows = lax.psum_scatter(part.astype(BF16), "dp", scatter_dimension=0, tiled=True)
        return lax.psum_scatter(rows, "z", scatter_dimension=0, tiled=True)

    gate_up_rows = reduce_rows(dot(ffn_in, gate_up_grad, 0, 0))
    down_rows = reduce_rows(dot(activated_low, branch_low, 0, 0))
    out_rows = lax.ppermute(reduce_rows(dot(attn_low, branch_attn)), ("dp", "x"), SWAP)
    qkv_rows = reduce_rows(dot(attn_in, qkv_pre, 0, 1))
    ctx = ("z", "x", "core")
    gate_up_all = lax.all_gather(gate_up_rows, ctx, axis=0).reshape(4, LINE, 64, 2, 4, 144)
    gate_up_all = gate_up_all.transpose(3, 0, 2, 4, 1, 5).reshape(2, 256, 4608).astype(F32)
    down_all = lax.all_gather(down_rows, ctx, axis=0).reshape(4, LINE, 36, 1024)
    down_all = down_all.transpose(1, 0, 2, 3).reshape(1152, 1024).astype(F32)
    out_all = lax.all_gather(out_rows, ctx, axis=0).reshape(4, 4, 2, 8, 1024)
    out_all = out_all.transpose(2, 1, 0, 3, 4).reshape(256, 1024).astype(F32)
    qkv_all = lax.all_gather(qkv_rows, ctx, axis=0).reshape(4, LINE, 64, 256)
    qkv_all = qkv_all.transpose(0, 2, 1, 3).reshape(256, LINE, 256).astype(F32)
    return (
        layer_out[None],
        input_grad[None],
        own_slice(0, 1024),
        qkv_all[:, :, 0:128].reshape(256, 1024),
        qkv_all[:, :, 128:192].reshape(256, 512),
        qkv_all[:, :, 192:256].reshape(256, 512),
        out_all,
        own_slice(2048, 64),
        own_slice(2112, 64),
        own_slice(1024, 1024),
        gate_up_all[0],
        gate_up_all[1],
        down_all,
    )


def solution(mesh):
    fine = Mesh(mesh.devices.reshape(4, 4, 4, 2), ("dp", "z", "x", "core"))
    ctx = ("z", "x", "core")
    rows = P("dp", ctx, None)
    in_specs = (
        rows,
        P("dp", ctx),
        P(),
        P("dp"),
        P("dp", None),
        P("dp", None),
        P("dp", None),
        P("dp", None),
        P("dp"),
        P("dp"),
        P("dp"),
        P("dp", None),
        P("dp", None),
        P("dp", None),
        rows,
    )
    out_specs = (
        rows,
        rows,
        P("dp"),
        P("dp", None),
        P("dp", None),
        P("dp", None),
        P("dp", None),
        P("dp"),
        P("dp"),
        P("dp"),
        P("dp", None),
        P("dp", None),
        P("dp", None),
    )
    return jax.shard_map(
        on_device, mesh=fine, in_specs=in_specs, out_specs=out_specs, check_vma=False
    )
```

```python
import functools

import jax
import jax.numpy as jnp
import numpy as np
from jax import lax
from jax.experimental import pallas as pl
from jax.experimental.pallas import tpu as pltpu
from jax.sharding import Mesh, PartitionSpec as P

HD = 64
BLK = 64
GROUPS = 8
HALF = 256
ROWS = 512
PIECE = 528

NORM_EPS = 1e-05
ROPE_BASE = 1000000.0
EXP2_SCALE = float(HD**-0.5 * np.log2(np.e))
SCORE_SCALE = HD**-0.5

F32 = jnp.float32
BF16 = jnp.bfloat16
VMEM = pl.BlockSpec(memory_space=pltpu.VMEM)
ANY = pl.BlockSpec(memory_space=pl.ANY)


def dot(left, right, left_dim=1, right_dim=0):
    return lax.dot_general(
        left, right, (((left_dim,), (right_dim,)), ((), ())), preferred_element_type=F32
    )


def rms_scale(values, gain):
    return values * lax.rsqrt(jnp.mean(values * values, axis=-1, keepdims=True) + NORM_EPS) * gain


def head_norm_rope(raw, gain, cosine, sine):
    scaled = (
        raw
        * lax.rsqrt(jnp.mean(raw * raw, axis=1, keepdims=True) + NORM_EPS)
        * gain[None, :, None]
    )
    front = scaled[:, : HD // 2]
    back = scaled[:, HD // 2 :]
    return jnp.concatenate([front * cosine - back * sine, back * cosine + front * sine], axis=1)


def scores_of(keys_t, queries_t):
    return dot(keys_t, queries_t, 0, 0)


def head_pair(ref, kv_head, cols):
    first = 2 * kv_head * HD
    return jnp.concatenate(
        [ref[first : first + HD, cols], ref[first + HD : first + 2 * HD, cols]], axis=1
    )


def attend_kernel(q_ref, kv_ref, qo_ref, ko_ref, mixed_ref, low_ref, log_ref):
    for half in range(2):
        cols = slice(half * HALF, (half + 1) * HALF)
        q_order = jnp.concatenate([qo_ref[:, cols]] * 2, axis=1)
        for kv_head in range(2):
            q_t = head_pair(q_ref, kv_head, cols)

            def group(g, carried):
                acc, total = carried
                for k_half in range(half + 1):
                    keys = slice(k_half * HALF, (k_half + 1) * HALF)
                    probs = jnp.exp2(
                        scores_of(kv_ref[g, kv_head, 0:HD, keys], q_t) * EXP2_SCALE
                    )
                    if k_half == half:
                        allowed = ko_ref[g, keys, :] <= q_order
                        probs = jnp.where(allowed, probs, 0.0)
                    total = total + jnp.sum(probs, axis=0, keepdims=True)
                    acc = acc + dot(kv_ref[g, kv_head, HD : 2 * HD, keys], probs.astype(BF16))
                return acc, total

            acc, total = lax.fori_loop(
                0,
                GROUPS,
                group,
                (jnp.zeros((HD, 2 * HALF), F32), jnp.zeros((1, 2 * HALF), F32)),
            )
            mixed = acc / total
            logs = jnp.log2(total)
            for head in range(2):
                at = 2 * kv_head + head
                rows = slice(at * HD, (at + 1) * HD)
                part = mixed[:, head * HALF : (head + 1) * HALF]
                mixed_ref[rows, cols] = part
                low_ref[rows, cols] = part.astype(BF16)
                log_ref[at : at + 1, cols] = logs[:, head * HALF : (head + 1) * HALF]


def attend(q_t, kv_all, q_order, k_order):
    return pl.pallas_call(
        attend_kernel,
        out_shape=(
            jax.ShapeDtypeStruct((4 * HD, ROWS), F32),
            jax.ShapeDtypeStruct((4 * HD, ROWS), BF16),
            jax.ShapeDtypeStruct((4, ROWS), F32),
        ),
        in_specs=[VMEM] * 4,
        out_specs=(VMEM,) * 3,
        compiler_params=pltpu.CompilerParams(vmem_limit_bytes=40 * 2**20),
        cost_estimate=pl.CostEstimate(
            flops=2 * 10**9, bytes_accessed=4 * 10**6, transcendentals=6 * 10**6
        ),
    )(q_t, kv_all, q_order, k_order)


def attend_back_kernel(
    q_ref, kv_ref, qo_ref, ko_ref, mixed_ref, log_ref, grad_ref, dq_ref, dkv_ref, dkv_acc
):
    dkv_acc[...] = jnp.zeros_like(dkv_acc)
    for half in range(2):
        cols = slice(half * HALF, (half + 1) * HALF)
        q_order = jnp.concatenate([qo_ref[:, cols]] * 2, axis=1)
        for kv_head in range(2):
            q_t = head_pair(q_ref, kv_head, cols)
            grad_t = head_pair(grad_ref, kv_head, cols)
            at = 2 * kv_head
            log_total = jnp.concatenate(
                [log_ref[at : at + 1, cols], log_ref[at + 1 : at + 2, cols]], axis=1
            )
            prob_dot = jnp.sum(
                head_pair(mixed_ref, kv_head, cols) * grad_t.astype(F32), axis=0, keepdims=True
            )

            def group(g, dq):
                for k_half in range(half + 1):
                    keys = slice(k_half * HALF, (k_half + 1) * HALF)
                    k_t = kv_ref[g, kv_head, 0:HD, keys]
                    v_t = kv_ref[g, kv_head, HD : 2 * HD, keys]
                    probs = jnp.exp2(scores_of(k_t, q_t) * EXP2_SCALE - log_total)
                    if k_half == half:
                        allowed = ko_ref[g, keys, :] <= q_order
                        probs = jnp.where(allowed, probs, 0.0)
                    dkv_acc[g, kv_head, HD : 2 * HD, keys] += dot(
                        grad_t, probs.astype(BF16), 1, 1
                    )
                    score_grad = (probs * (scores_of(v_t, grad_t) - prob_dot)).astype(BF16)
                    dkv_acc[g, kv_head, 0:HD, keys] += dot(q_t, score_grad, 1, 1)
                    dq = dq + dot(k_t, score_grad)
                return dq

            dq = lax.fori_loop(0, GROUPS, group, jnp.zeros((HD, 2 * HALF), F32))
            for head in range(2):
                rows = slice((at + head) * HD, (at + head + 1) * HD)
                dq_ref[rows, cols] = dq[:, head * HALF : (head + 1) * HALF] * SCORE_SCALE

    def finish(g, unused):
        for kv_head in range(2):
            dkv_ref[g, kv_head, 0:HD, :] = (dkv_acc[g, kv_head, 0:HD, :] * SCORE_SCALE).astype(
                BF16
            )
            dkv_ref[g, kv_head, HD : 2 * HD, :] = dkv_acc[g, kv_head, HD : 2 * HD, :].astype(BF16)
        return unused

    lax.fori_loop(0, GROUPS, finish, 0)


def attend_back(q_t, kv_all, q_order, k_order, mixed, log_total, mixed_grad):
    return pl.pallas_call(
        attend_back_kernel,
        out_shape=(
            jax.ShapeDtypeStruct((4 * HD, ROWS), F32),
            jax.ShapeDtypeStruct((GROUPS, 2, 2 * HD, ROWS), BF16),
        ),
        in_specs=[VMEM] * 7,
        out_specs=(VMEM,) * 2,
        scratch_shapes=[pltpu.VMEM((GROUPS, 2, 2 * HD, ROWS), F32)],
        compiler_params=pltpu.CompilerParams(vmem_limit_bytes=40 * 2**20),
        cost_estimate=pl.CostEstimate(
            flops=4 * 10**9, bytes_accessed=6 * 10**6, transcendentals=6 * 10**6
        ),
    )(q_t, kv_all, q_order, k_order, mixed, log_total, mixed_grad)


def ring(axis):
    me = lax.axis_index(axis)
    return me, lax.rem(me + 1, 4), lax.rem(me + 2, 4), lax.rem(me + 3, 4)


def meet(partners):
    barrier = pltpu.get_barrier_semaphore()
    for partner in partners:
        pl.semaphore_signal(
            barrier, inc=1, device_id=partner, device_id_type=pl.DeviceIdType.MESH
        )
    pl.semaphore_wait(barrier, len(partners))


class Sends:
    def __init__(self, send_sems, recv_sems):
        self.send_sems, self.recv_sems, self.started = send_sems, recv_sems, []

    def __call__(self, source, target, partner):
        at = len(self.started)
        copy = pltpu.make_async_remote_copy(
            src_ref=source,
            dst_ref=target,
            send_sem=self.send_sems.at[at],
            recv_sem=self.recv_sems.at[at],
            device_id=partner,
            device_id_type=pl.DeviceIdType.MESH,
        )
        copy.start()
        self.started.append(copy)
        return copy

    def finish(self):
        for copy in self.started:
            copy.wait_send()


def gather_kernel(axis, sibling, at, src, out, send_sems, recv_sems, local_sems):
    me, right, far, left = ring(axis)
    core = lax.axis_index("core")
    to_right, to_left, to_sib = {axis: right}, {axis: left}, {"core": 1 - core}
    meet([to_right, to_left] + ([to_sib] if sibling else []))
    send = Sends(send_sems, recv_sems)
    from_sib = []

    def share(place, half, source=None):
        if sibling:
            target = at(out, place, core, half)
            from_sib.append(send(target if source is None else source, target, to_sib))

    def own_to(half, partner):
        return send(src.at[half], at(out, me, core, half), partner)

    right0 = own_to(0, to_right)
    left1 = own_to(1, to_left)
    right1 = own_to(1, to_right)
    left0 = own_to(0, to_left)
    own = [
        pltpu.make_async_copy(src.at[h], at(out, me, core, h), local_sems.at[h]) for h in range(2)
    ]
    for copy in own:
        copy.start()
    for h in range(2):
        share(me, h, src.at[h])
    right0.wait_recv()
    far0 = send(at(out, left, core, 0), at(out, left, core, 0), to_right)
    share(left, 0)
    left1.wait_recv()
    far1 = send(at(out, right, core, 1), at(out, right, core, 1), to_left)
    share(right, 1)
    right1.wait_recv()
    share(left, 1)
    left0.wait_recv()
    share(right, 0)
    far0.wait_recv()
    share(far, 0)
    far1.wait_recv()
    share(far, 1)
    for copy in from_sib:
        copy.wait_recv()
    for copy in own:
        copy.wait()
    send.finish()


def gather_call(kernel_id, axis, sibling, at, src, out_shape):
    return pl.pallas_call(
        functools.partial(gather_kernel, axis, sibling, at),
        out_shape=jax.ShapeDtypeStruct(out_shape, BF16),
        in_specs=[ANY],
        out_specs=ANY,
        scratch_shapes=[
            pltpu.SemaphoreType.DMA((14 if sibling else 6,)),
            pltpu.SemaphoreType.DMA((14 if sibling else 6,)),
            pltpu.SemaphoreType.DMA((2,)),
        ],
        compiler_params=pltpu.CompilerParams(collective_id=kernel_id, has_side_effects=True),
    )(src)


def line_gather(kernel_id, rows):
    width = rows.shape[1]
    gathered = gather_call(
        kernel_id,
        "x",
        False,
        lambda out, place, core, half: out.at[half, place],
        rows.reshape(2, BLK, width),
        (2, 4, BLK, width),
    )
    return gathered.reshape(ROWS, width)


def sequence_gather(kernel_id, kv):
    gathered = gather_call(
        kernel_id,
        "z",
        True,
        lambda out, place, core, half: out.at[place, core, half],
        kv,
        (4, 2, 2, 2 * HD, ROWS),
    )
    return gathered.reshape(GROUPS, 2, 2 * HD, ROWS)


def add_low(left, right):
    return (left.astype(F32) + right.astype(F32)).astype(BF16)


def line_scatter_kernel(part, out, pair, self_rows, far_in, left_in, right_in, sends, recvs, loads):
    me, right, far, left = ring("x")
    to_right, to_left = {"x": right}, {"x": left}
    local = [
        pltpu.make_async_copy(part.at[0, right], pair.at[0], loads.at[0]),
        pltpu.make_async_copy(part.at[1, left], pair.at[1], loads.at[1]),
        pltpu.make_async_copy(part.at[0, me], self_rows.at[0], loads.at[2]),
        pltpu.make_async_copy(part.at[1, me], self_rows.at[1], loads.at[3]),
    ]
    for copy in local:
        copy.start()
    meet([to_right, to_left])
    send = Sends(sends, recvs)
    far0 = send(part.at[0, far], far_in.at[0], to_right)
    far1 = send(part.at[1, far], far_in.at[1], to_left)
    right1 = send(part.at[1, right], left_in.at[1], to_right)
    left0 = send(part.at[0, left], right_in.at[0], to_left)
    local[0].wait()
    far0.wait_recv()
    pair[0] = add_low(pair[0], far_in[0])
    right0 = send(pair.at[0], left_in.at[0], to_right)
    local[1].wait()
    far1.wait_recv()
    pair[1] = add_low(pair[1], far_in[1])
    left1 = send(pair.at[1], right_in.at[1], to_left)
    local[2].wait()
    local[3].wait()
    right1.wait_recv()
    left0.wait_recv()
    right0.wait_recv()
    left1.wait_recv()
    for h in range(2):
        out[h] = (
            self_rows[h].astype(F32) + left_in[h].astype(F32) + right_in[h].astype(F32)
        )
    send.finish()


def line_scatter(kernel_id, partial):
    width = partial.shape[1]
    buffer = pltpu.VMEM((2, BLK, width), BF16)
    return pl.pallas_call(
        line_scatter_kernel,
        out_shape=jax.ShapeDtypeStruct((2, BLK, width), F32),
        in_specs=[ANY],
        out_specs=VMEM,
        scratch_shapes=[buffer] * 5
        + [
            pltpu.SemaphoreType.DMA((6,)),
            pltpu.SemaphoreType.DMA((6,)),
            pltpu.SemaphoreType.DMA((4,)),
        ],
        compiler_params=pltpu.CompilerParams(
            collective_id=kernel_id, has_side_effects=True, vmem_limit_bytes=32 * 2**20
        ),
    )(partial.reshape(2, 4, BLK, width)).reshape(2 * BLK, width)


class RingSum:
    def __init__(self, send, axis, chunk, far_in, left_in, right_in):
        self.send, self.chunk = send, chunk
        self.far_in, self.left_in, self.right_in = far_in, left_in, right_in
        self.me, self.right, self.far, self.left = ring(axis)
        self.to_right, self.to_left = {axis: self.right}, {axis: self.left}

    def begin(self):
        send, chunk = self.send, self.chunk
        self.far0 = send(chunk(self.far, 0), self.far_in(0), self.to_right)
        self.far1 = send(chunk(self.far, 1), self.far_in(1), self.to_left)
        self.right1 = send(chunk(self.right, 1), self.left_in(1), self.to_right)
        self.left0 = send(chunk(self.left, 0), self.right_in(0), self.to_left)

    def middle(self):
        send, chunk = self.send, self.chunk
        self.far0.wait_recv()
        mine = chunk(self.right, 0)
        mine[...] = add_low(mine[...], self.far_in(0)[...])
        self.right0 = send(mine, self.left_in(0), self.to_right)
        self.far1.wait_recv()
        mine = chunk(self.left, 1)
        mine[...] = add_low(mine[...], self.far_in(1)[...])
        self.left1 = send(mine, self.right_in(1), self.to_left)

    def end(self, store):
        self.right1.wait_recv()
        self.left0.wait_recv()
        self.right0.wait_recv()
        self.left1.wait_recv()
        for h in range(2):
            store(
                h,
                self.chunk(self.me, h)[...].astype(F32)
                + self.left_in(h)[...].astype(F32)
                + self.right_in(h)[...].astype(F32),
            )


def sequence_scatter_kernel(
    part, out, own, other, far_in, left_in, right_in, sends, recvs, loads
):
    core = lax.axis_index("core")
    me, right, far, left = ring("z")
    order = (far, right, left, me)
    local = [
        pltpu.make_async_copy(part.at[place, core], own.at[place], loads.at[i])
        for i, place in enumerate(order)
    ]
    for copy in local:
        copy.start()
    to_sib = {"core": 1 - core}
    meet([{"z": right}, {"z": left}, to_sib])
    send = Sends(sends, recvs)
    shared = [send(part.at[place, 1 - core], other.at[place], to_sib) for place in order]

    def merge(i):
        local[i].wait()
        shared[i].wait_recv()
        own[order[i]] = add_low(own[order[i]], other[order[i]])

    ring_sum = RingSum(
        send,
        "z",
        lambda place, h: own.at[place, h],
        lambda h: far_in.at[h],
        lambda h: left_in.at[h],
        lambda h: right_in.at[h],
    )
    for i in range(3):
        merge(i)
    ring_sum.begin()
    merge(3)
    ring_sum.middle()

    def store(h, value):
        out[h] = value

    ring_sum.end(store)
    send.finish()


def sequence_scatter(kernel_id, partial):
    buffer = pltpu.VMEM((2, 2 * HD, ROWS), BF16)
    wide = pltpu.VMEM((4, 2, 2 * HD, ROWS), BF16)
    return pl.pallas_call(
        sequence_scatter_kernel,
        out_shape=jax.ShapeDtypeStruct((2, 2 * HD, ROWS), F32),
        in_specs=[ANY],
        out_specs=VMEM,
        scratch_shapes=[wide, wide, buffer, buffer, buffer]
        + [
            pltpu.SemaphoreType.DMA((10,)),
            pltpu.SemaphoreType.DMA((10,)),
            pltpu.SemaphoreType.DMA((4,)),
        ],
        compiler_params=pltpu.CompilerParams(
            collective_id=kernel_id, has_side_effects=True, vmem_limit_bytes=32 * 2**20
        ),
    )(partial.reshape(4, 2, 2, 2 * HD, ROWS))


def grads_kernel(
    gu, qkv, down, out, result,
    gu_own, gu_sib, qkv_own, qkv_sib, down_own, down_sib, out_own, out_sib,
    packed, far_a, left_a, right_a, mid, far_b, left_b, right_b,
    sends, recvs, loads,
):
    core = lax.axis_index("core")
    me_y, right_y, far_y, left_y = ring("dp")
    me_z, right_z, far_z, left_z = ring("z")
    to_sib = {"core": 1 - core}
    views = [
        (lambda c: gu.at[:, :, c], gu_own, gu_sib),
        (lambda c: qkv.at[:, :, c], qkv_own, qkv_sib),
        (lambda c: down.at[:, c], down_own, down_sib),
        (lambda c: out.at[:, c], out_own, out_sib),
    ]
    local = [
        pltpu.make_async_copy(view(core), mine, loads.at[i])
        for i, (view, mine, unused) in enumerate(views)
    ]
    for copy in local:
        copy.start()
    meet([{"dp": right_y}, {"dp": left_y}, {"z": right_z}, {"z": left_z}, to_sib])
    send = Sends(sends, recvs)
    shared = [send(view(1 - core), theirs, to_sib) for view, unused, theirs in views]
    for copy in local:
        copy.wait()
    for copy in shared:
        copy.wait_recv()

    def pack(y, unused):
        for z in range(4):
            for s in range(2):
                for t in range(9):
                    cols = slice(s * 1152 + t * 128, s * 1152 + (t + 1) * 128)
                    packed[s, y, z, t * 32 : (t + 1) * 32, :] = add_low(
                        gu_own[y, z, :, cols], gu_sib[y, z, :, cols]
                    )
                for t in range(2):
                    cols = slice(s * 256 + t * 128, s * 256 + (t + 1) * 128)
                    packed[s, y, z, 288 + t * 32 : 320 + t * 32, :] = add_low(
                        qkv_own[y, z, :, cols], qkv_sib[y, z, :, cols]
                    )
                cols = slice(s * 512 + z * 128, s * 512 + (z + 1) * 128)
                packed[s, y, z, 352:496, :] = add_low(down_own[y, :, cols], down_sib[y, :, cols])
                packed[s, y, z, 496:528, :] = add_low(out_own[y, :, cols], out_sib[y, :, cols])
        return unused

    lax.fori_loop(0, 4, pack, 0)

    two = (pl.ds(0, 2), pl.ds(2, 2))
    rows = (pl.ds(0, 272), pl.ds(272, 256))
    first = [
        RingSum(
            send,
            "dp",
            lambda place, h: packed.at[0, place, two[h]],
            lambda h: far_a.at[0, h],
            lambda h: left_a.at[0, h],
            lambda h: right_a.at[0, h],
        ),
        RingSum(
            send,
            "z",
            lambda place, h: packed.at[1, two[h], place],
            lambda h: far_a.at[1, h],
            lambda h: left_a.at[1, h],
            lambda h: right_a.at[1, h],
        ),
    ]
    second = [
        RingSum(
            send,
            axis,
            lambda place, h, s=s: mid.at[s, place, rows[h]],
            lambda h, s=s: far_b.at[s, rows[h]],
            lambda h, s=s: left_b.at[s, rows[h]],
            lambda h, s=s: right_b.at[s, rows[h]],
        )
        for s, axis in enumerate(("z", "dp"))
    ]
    for step in first:
        step.begin()
    for step in first:
        step.middle()
    for s in range(2):

        def keep(h, value, s=s):
            mid[s, 2 * h : 2 * h + 2] = value.astype(BF16)

        first[s].end(keep)
        second[s].begin()
    for step in second:
        step.middle()
    for s in range(2):

        def keep_last(h, value, s=s):
            result[s, rows[h], :] = value.astype(BF16)

        second[s].end(keep_last)
    send.finish()


def sum_grads(kernel_id, gu, qkv, down, out):
    def vm(*shape):
        return pltpu.VMEM(shape, BF16)

    return pl.pallas_call(
        grads_kernel,
        out_shape=jax.ShapeDtypeStruct((2, PIECE, 128), BF16),
        in_specs=[ANY] * 4,
        out_specs=VMEM,
        scratch_shapes=[
            vm(4, 4, 32, 2304), vm(4, 4, 32, 2304),
            vm(4, 4, 32, 512), vm(4, 4, 32, 512),
            vm(4, 144, 1024), vm(4, 144, 1024),
            vm(4, 32, 1024), vm(4, 32, 1024),
            vm(2, 4, 4, PIECE, 128),
            vm(2, 2, 2, PIECE, 128), vm(2, 2, 2, PIECE, 128), vm(2, 2, 2, PIECE, 128),
            vm(2, 4, PIECE, 128),
            vm(2, PIECE, 128), vm(2, PIECE, 128), vm(2, PIECE, 128),
            pltpu.SemaphoreType.DMA((28,)),
            pltpu.SemaphoreType.DMA((28,)),
            pltpu.SemaphoreType.DMA((4,)),
        ],
        compiler_params=pltpu.CompilerParams(
            collective_id=kernel_id, has_side_effects=True, vmem_limit_bytes=48 * 2**20
        ),
    )(
        gu.reshape(4, 4, 2, 32, 2304),
        qkv.reshape(4, 4, 2, 32, 512),
        down.reshape(4, 2, 144, 1024),
        out.reshape(4, 2, 32, 1024),
    )


class RingCopy:
    def __init__(self, send, axis, place_of):
        self.send, self.at = send, place_of
        self.me, self.right, self.far, self.left = ring(axis)
        self.to_right, self.to_left = {axis: self.right}, {axis: self.left}

    def begin(self):
        me = self.me
        self.right0 = self.send(self.at(me, 0), self.at(me, 0), self.to_right)
        self.left1 = self.send(self.at(me, 1), self.at(me, 1), self.to_left)
        self.right1 = self.send(self.at(me, 1), self.at(me, 1), self.to_right)
        self.left0 = self.send(self.at(me, 0), self.at(me, 0), self.to_left)

    def middle(self):
        self.right0.wait_recv()
        self.far0 = self.send(self.at(self.left, 0), self.at(self.left, 0), self.to_right)
        self.left1.wait_recv()
        self.far1 = self.send(self.at(self.right, 1), self.at(self.right, 1), self.to_left)

    def near(self):
        self.right1.wait_recv()
        self.left0.wait_recv()

    def end(self):
        self.far0.wait_recv()
        self.far1.wait_recv()


def spread_kernel(piece, out, sends, recvs, loads):
    core = lax.axis_index("core")
    me_x, right_x, far_x, left_x = ring("x")
    me_z, right_z, far_z, left_z = ring("z")
    to_sib = {"core": 1 - core}
    own = [
        pltpu.make_async_copy(piece.at[s], out.at[s, core, me_z, me_x], loads.at[s])
        for s in range(2)
    ]
    for copy in own:
        copy.start()
    meet([{"x": right_x}, {"x": left_x}, {"z": right_z}, {"z": left_z}, to_sib])
    send = Sends(sends, recvs)
    rows = (pl.ds(0, 272), pl.ds(272, 256))
    two = (pl.ds(0, 2), pl.ds(2, 2))
    first = [
        RingCopy(send, "z", lambda place, h: out.at[0, core, place, me_x, rows[h]]),
        RingCopy(send, "x", lambda place, h: out.at[1, core, me_z, place, rows[h]]),
    ]
    second = [
        RingCopy(send, "x", lambda place, h: out.at[0, core, two[h], place]),
        RingCopy(send, "z", lambda place, h: out.at[1, core, place, two[h]]),
    ]
    for copy in own:
        copy.wait()
    for step in first:
        step.begin()
    for step in first:
        step.middle()
    for s in range(2):
        first[s].near()
        first[s].end()
        second[s].begin()
    shared = []

    def share(view):
        shared.append(send(view, view, to_sib))

    share(out.at[0, core, :, me_x])
    share(out.at[1, core, me_z])
    for step in second:
        step.middle()
    for s in range(2):
        second[s].near()
        if s == 0:
            share(out.at[0, core, :, left_x])
            share(out.at[0, core, :, right_x])
        else:
            share(out.at[1, core, left_z])
            share(out.at[1, core, right_z])
    for s in range(2):
        second[s].end()
        share(out.at[0, core, :, far_x] if s == 0 else out.at[1, core, far_z])
    for copy in shared:
        copy.wait_recv()
    send.finish()


def spread(kernel_id, piece):
    return pl.pallas_call(
        spread_kernel,
        out_shape=jax.ShapeDtypeStruct((2, 2, 4, 4, PIECE, 128), BF16),
        in_specs=[ANY],
        out_specs=ANY,
        scratch_shapes=[
            pltpu.SemaphoreType.DMA((32,)),
            pltpu.SemaphoreType.DMA((32,)),
            pltpu.SemaphoreType.DMA((2,)),
        ],
        compiler_params=pltpu.CompilerParams(collective_id=kernel_id, has_side_effects=True),
    )(piece)


def unpack_rows_kernel(pieces, gate, up, query, key, value):
    for x in range(4):
        for t in range(9):
            cols = slice(x * 1152 + t * 128, x * 1152 + (t + 1) * 128)
            gate[:, cols] = pieces[0, 0, 0, x, t * 32 : (t + 1) * 32, :].astype(F32)
            up[:, cols] = pieces[1, 0, 0, x, t * 32 : (t + 1) * 32, :].astype(F32)
        for t in range(2):
            cols = slice(x * 256 + t * 128, x * 256 + (t + 1) * 128)
            query[:, cols] = pieces[0, 0, 0, x, 288 + t * 32 : 320 + t * 32, :].astype(F32)
        cols = slice(x * 128, (x + 1) * 128)
        key[:, cols] = pieces[1, 0, 0, x, 288:320, :].astype(F32)
        value[:, cols] = pieces[1, 0, 0, x, 320:352, :].astype(F32)


def unpack_columns_kernel(pieces, down, out):
    for s in range(2):
        for z in range(4):
            cols = slice(s * 512 + z * 128, s * 512 + (z + 1) * 128)
            down[:, cols] = pieces[s, 0, z, 0, 352:496, :].astype(F32)
            out[:, cols] = pieces[s, 0, z, 0, 496:528, :].astype(F32)


def unpack(pieces):
    rows = pl.pallas_call(
        unpack_rows_kernel,
        grid=(4, 2),
        out_shape=tuple(
            jax.ShapeDtypeStruct((256, width), F32) for width in (4608, 4608, 1024, 512, 512)
        ),
        in_specs=[pl.BlockSpec((2, 1, 1, 4, PIECE, 128), lambda z, c: (0, c, z, 0, 0, 0))],
        out_specs=tuple(
            pl.BlockSpec((32, width), lambda z, c: (2 * z + c, 0))
            for width in (4608, 4608, 1024, 512, 512)
        ),
        compiler_params=pltpu.CompilerParams(vmem_limit_bytes=32 * 2**20),
    )(pieces)
    columns = pl.pallas_call(
        unpack_columns_kernel,
        grid=(4, 2),
        out_shape=(
            jax.ShapeDtypeStruct((1152, 1024), F32),
            jax.ShapeDtypeStruct((256, 1024), F32),
        ),
        in_specs=[pl.BlockSpec((2, 1, 4, 1, PIECE, 128), lambda x, c: (0, c, 0, x, 0, 0))],
        out_specs=(
            pl.BlockSpec((144, 1024), lambda x, c: (2 * x + c, 0)),
            pl.BlockSpec((32, 1024), lambda x, c: (2 * x + c, 0)),
        ),
        compiler_params=pltpu.CompilerParams(vmem_limit_bytes=32 * 2**20),
    )(pieces)
    return rows + columns


SWAP = [(a * 4 + b, b * 4 + a) for a in range(4) for b in range(4)]


def on_device(
    hidden_in,
    positions,
    block_of,
    attn_gain,
    query_weight,
    key_weight,
    value_weight,
    out_weight,
    query_gain,
    key_gain,
    ffn_gain,
    gate_weight,
    up_weight,
    down_weight,
    cotangent,
):
    z_at = lax.axis_index("z")
    x_at = lax.axis_index("x")
    core_at = lax.axis_index("core")
    dp_at = lax.axis_index("dp")

    hidden_rows = hidden_in[0]
    grad_rows = cotangent[0]

    in_block = jnp.arange(BLK, dtype=jnp.int32)
    blocks = block_of.reshape(4, 4, 2, 2).transpose(0, 2, 3, 1)
    order_all = (blocks[..., None] * BLK + in_block).reshape(GROUPS, ROWS)
    own_order = lax.dynamic_index_in_dim(order_all, z_at * 2 + core_at, 0, keepdims=True)
    k_order = order_all.reshape(GROUPS, ROWS, 1)
    own_slot = 2 * (z_at * 8 + x_at * 2 + core_at)
    first_block = lax.dynamic_index_in_dim(block_of, own_slot, 0, keepdims=False)
    offset = positions[0, 0] - first_block * BLK
    frequency = ROPE_BASE ** (-2.0 * jnp.arange(HD // 2, dtype=F32) / HD)
    angles = (own_order + offset).astype(F32) * frequency[:, None]
    cosine, sine = jnp.cos(angles), jnp.sin(angles)

    def columns(weight, width):
        return lax.dynamic_slice_in_dim(weight, x_at * width, width, axis=1)

    def swapped_rows(weight, rows):
        own = lax.dynamic_slice_in_dim(weight, x_at * rows, rows, axis=0)
        return lax.all_gather(lax.ppermute(own, ("dp", "x"), SWAP), "dp", axis=0, tiled=True)

    gains = lax.all_gather(
        jnp.concatenate([attn_gain, ffn_gain, query_gain, key_gain]), "dp", axis=0
    ).astype(F32)
    attn_gain_all = gains[:, 0:256].reshape(1024)
    ffn_gain_all = gains[:, 256:512].reshape(1024)
    query_gain_all = gains[:, 512:528].reshape(HD)
    key_gain_all = gains[:, 528:544].reshape(HD)
    qkv_weight = lax.all_gather(
        jnp.concatenate(
            [columns(query_weight, 256), columns(key_weight, 128), columns(value_weight, 128)],
            axis=1,
        ),
        "dp",
        axis=0,
        tiled=True,
    )
    out_slice = swapped_rows(out_weight, 64)
    gate_up = lax.all_gather(
        jnp.concatenate([columns(gate_weight, 1152), columns(up_weight, 1152)], axis=1),
        "dp",
        axis=0,
        tiled=True,
    )
    down_slice = swapped_rows(down_weight, 288)

    hidden = hidden_rows.astype(F32)
    line_rows = line_gather(0, jnp.concatenate([hidden_rows, grad_rows], axis=1))
    line_hidden = line_rows[:, 0:1024]
    branch_low = line_rows[:, 1024:2048]
    attn_in = rms_scale(line_hidden.astype(F32), attn_gain_all).astype(BF16)
    qkv_t = dot(qkv_weight, attn_in, 0, 1)
    q_rot, q_back = jax.vjp(
        lambda r, g: head_norm_rope(r, g, cosine, sine),
        qkv_t[0:256].reshape(4, HD, ROWS),
        query_gain_all,
    )
    k_rot, k_back = jax.vjp(
        lambda r, g: head_norm_rope(r, g, cosine, sine),
        qkv_t[256:384].reshape(2, HD, ROWS),
        key_gain_all,
    )
    q_low = q_rot.reshape(4 * HD, ROWS).astype(BF16)
    kv_low = jnp.concatenate([k_rot, qkv_t[384:512].reshape(2, HD, ROWS)], axis=1).astype(BF16)
    kv_all = sequence_gather(1, kv_low)
    mixed, attn_low, log_total = attend(q_low, kv_all, own_order, k_order)
    after_attn = hidden + line_scatter(2, dot(attn_low, out_slice, 0, 0).astype(BF16))
    normed_ffn, norm_ffn_back = jax.vjp(rms_scale, after_attn, ffn_gain_all)
    ffn_in = line_gather(3, normed_ffn.astype(BF16))
    gate_up_proj = dot(ffn_in, gate_up)
    gate_proj = gate_up_proj[:, :1152]
    up_proj = gate_up_proj[:, 1152:]
    activated, swiglu_back = jax.vjp(lambda g, u: jax.nn.silu(g) * u, gate_proj, up_proj)
    activated_low = activated.astype(BF16)
    layer_out = (
        after_attn + line_scatter(4, dot(activated_low, down_slice).astype(BF16))
    ).astype(BF16)

    residual_grad = grad_rows.astype(F32)
    activated_grad = dot(branch_low, down_slice, 1, 1)
    gate_grad, up_grad = swiglu_back(activated_grad)
    gate_up_grad = jnp.concatenate([gate_grad, up_grad], axis=1).astype(BF16)
    ffn_in_grad = line_scatter(5, dot(gate_up_grad, gate_up, 1, 1).astype(BF16))
    mid_part, ffn_gain_part = norm_ffn_back(ffn_in_grad)
    mid_grad = residual_grad + mid_part
    branch_attn = line_gather(6, mid_grad.astype(BF16))
    mixed_grad = dot(out_slice, branch_attn, 1, 1).astype(BF16)
    q_grad, kv_grad_all = attend_back(
        q_low, kv_all, own_order, k_order, mixed, log_total, mixed_grad
    )
    kv_grad = sequence_scatter(7, kv_grad_all)
    q_pre, q_gain_part = q_back(q_grad.reshape(4, HD, ROWS))
    k_pre, k_gain_part = k_back(kv_grad[:, 0:HD])
    qkv_pre = jnp.concatenate(
        [
            q_pre.reshape(4 * HD, ROWS),
            k_pre.reshape(2 * HD, ROWS),
            kv_grad[:, HD:].reshape(2 * HD, ROWS),
        ],
        axis=0,
    ).astype(BF16)
    attn_in_grad = line_scatter(8, dot(qkv_pre, qkv_weight, 0, 1).astype(BF16))
    unused, norm_attn_back = jax.vjp(rms_scale, hidden, attn_gain_all)
    hidden_part, attn_gain_part = norm_attn_back(attn_in_grad)
    input_grad = (mid_grad + hidden_part).astype(BF16)

    gain_sums = lax.psum(
        jnp.concatenate([attn_gain_part, ffn_gain_part, q_gain_part, k_gain_part]),
        ("dp", "z", "x", "core"),
    )

    def own_slice(begin, size):
        return lax.dynamic_slice_in_dim(
            gain_sums[begin : begin + size], dp_at * (size // 4), size // 4
        )

    own_piece = sum_grads(
        9,
        dot(ffn_in, gate_up_grad, 0, 0).astype(BF16),
        dot(attn_in, qkv_pre, 0, 1).astype(BF16),
        dot(activated_low, branch_low, 0, 0).astype(BF16),
        dot(attn_low, branch_attn).astype(BF16),
    )
    swapped = lax.ppermute(own_piece[:, 352:], ("dp", "x"), SWAP)
    pieces = spread(10, jnp.concatenate([own_piece[:, :352], swapped], axis=1))
    gate_all, up_all, query_all, key_all, value_all, down_all, out_all = unpack(pieces)
    return (
        layer_out[None],
        input_grad[None],
        own_slice(0, 1024),
        query_all,
        key_all,
        value_all,
        out_all,
        own_slice(2048, 64),
        own_slice(2112, 64),
        own_slice(1024, 1024),
        gate_all,
        up_all,
        down_all,
    )


def solution(mesh):
    fine = Mesh(mesh.devices.reshape(4, 4, 4, 2), ("dp", "z", "x", "core"))
    ctx = ("z", "x", "core")
    rows = P("dp", ctx, None)
    vector, matrix = P("dp"), P("dp", None)
    return jax.shard_map(
        on_device,
        mesh=fine,
        in_specs=(rows, P("dp", ctx), P(), vector)
        + (matrix,) * 4
        + (vector,) * 3
        + (matrix,) * 3
        + (rows,),
        out_specs=(rows, rows, vector) + (matrix,) * 4 + (vector,) * 3 + (matrix,) * 3,
        check_vma=False,
    )
```

```python
import functools

import jax
import jax.numpy as jnp
import numpy as np
from jax import lax
from jax.experimental import pallas as pl
from jax.experimental.pallas import tpu as pltpu
from jax.sharding import Mesh, PartitionSpec as P

HD = 64
BLK = 64
GROUPS = 8
HALF = 256
ROWS = 512
FF_PIECE = 432
PIECE = 96

NORM_EPS = 1e-05
ROPE_BASE = 1000000.0
EXP2_SCALE = float(HD**-0.5 * np.log2(np.e))
SCORE_SCALE = HD**-0.5

F32 = jnp.float32
BF16 = jnp.bfloat16
VMEM = pl.BlockSpec(memory_space=pltpu.VMEM)
ANY = pl.BlockSpec(memory_space=pl.ANY)


def dot(left, right, left_dim=1, right_dim=0):
    return lax.dot_general(
        left, right, (((left_dim,), (right_dim,)), ((), ())), preferred_element_type=F32
    )


def rms_scale(values, gain):
    return values * lax.rsqrt(jnp.mean(values * values, axis=-1, keepdims=True) + NORM_EPS) * gain


def head_norm_rope(raw, gain, cosine, sine):
    scaled = (
        raw
        * lax.rsqrt(jnp.mean(raw * raw, axis=1, keepdims=True) + NORM_EPS)
        * gain[None, :, None]
    )
    front = scaled[:, : HD // 2]
    back = scaled[:, HD // 2 :]
    return jnp.concatenate([front * cosine - back * sine, back * cosine + front * sine], axis=1)


def scores_of(keys_t, queries_t):
    return dot(keys_t, queries_t, 0, 0)


def head_pair(ref, kv_head, cols):
    first = 2 * kv_head * HD
    return jnp.concatenate(
        [ref[first : first + HD, cols], ref[first + HD : first + 2 * HD, cols]], axis=1
    )


def attend_kernel(q_ref, kv_ref, qo_ref, ko_ref, mixed_ref, low_ref, log_ref):
    for half in range(2):
        cols = slice(half * HALF, (half + 1) * HALF)
        q_order = jnp.concatenate([qo_ref[:, cols]] * 2, axis=1)
        queries = [head_pair(q_ref, kv_head, cols) for kv_head in range(2)]

        def group(g, carried):
            carried = list(carried)
            for k_half in range(half + 1):
                keys = slice(k_half * HALF, (k_half + 1) * HALF)
                for kv_head in range(2):
                    acc, total = carried[kv_head]
                    probs = jnp.exp2(
                        scores_of(kv_ref[g, kv_head, 0:HD, keys], queries[kv_head]) * EXP2_SCALE
                    )
                    if k_half == half:
                        allowed = ko_ref[g, keys, :] <= q_order
                        probs = jnp.where(allowed, probs, 0.0)
                    total = total + jnp.sum(probs, axis=0, keepdims=True)
                    acc = acc + dot(kv_ref[g, kv_head, HD : 2 * HD, keys], probs.astype(BF16))
                    carried[kv_head] = (acc, total)
            return tuple(carried)

        start = (jnp.zeros((HD, 2 * HALF), F32), jnp.zeros((1, 2 * HALF), F32))
        sums = lax.fori_loop(0, GROUPS, group, (start, start))
        for kv_head, (acc, total) in enumerate(sums):
            mixed = acc / total
            logs = jnp.log2(total)
            for head in range(2):
                at = 2 * kv_head + head
                rows = slice(at * HD, (at + 1) * HD)
                part = mixed[:, head * HALF : (head + 1) * HALF]
                mixed_ref[rows, cols] = part
                low_ref[rows, cols] = part.astype(BF16)
                log_ref[at : at + 1, cols] = logs[:, head * HALF : (head + 1) * HALF]


def attend(q_t, kv_all, q_order, k_order):
    return pl.pallas_call(
        attend_kernel,
        out_shape=(
            jax.ShapeDtypeStruct((4 * HD, ROWS), F32),
            jax.ShapeDtypeStruct((4 * HD, ROWS), BF16),
            jax.ShapeDtypeStruct((4, ROWS), F32),
        ),
        in_specs=[VMEM] * 4,
        out_specs=(VMEM,) * 3,
        compiler_params=pltpu.CompilerParams(vmem_limit_bytes=40 * 2**20),
        cost_estimate=pl.CostEstimate(
            flops=2 * 10**9, bytes_accessed=4 * 10**6, transcendentals=6 * 10**6
        ),
    )(q_t, kv_all, q_order, k_order)


def ring(axis):
    me = lax.axis_index(axis)
    return me, lax.rem(me + 1, 4), lax.rem(me + 2, 4), lax.rem(me + 3, 4)


def meet(partners):
    barrier = pltpu.get_barrier_semaphore()
    for partner in partners:
        pl.semaphore_signal(
            barrier, inc=1, device_id=partner, device_id_type=pl.DeviceIdType.MESH
        )
    pl.semaphore_wait(barrier, len(partners))


class Sends:
    def __init__(self, send_sems, recv_sems):
        self.send_sems, self.recv_sems, self.started = send_sems, recv_sems, []

    def __call__(self, source, target, partner):
        at = len(self.started)
        copy = pltpu.make_async_remote_copy(
            src_ref=source,
            dst_ref=target,
            send_sem=self.send_sems.at[at],
            recv_sem=self.recv_sems.at[at],
            device_id=partner,
            device_id_type=pl.DeviceIdType.MESH,
        )
        copy.start()
        self.started.append(copy)
        return copy

    def finish(self):
        for copy in self.started:
            copy.wait_send()


class RingGather:
    def __init__(self, send, axis, at, own, sibling=False, share_own=False):
        self.send, self.axis, self.own = send, axis, own
        self.me, self.right, self.far, self.left = ring(axis)
        self.to_right, self.to_left = {axis: self.right}, {axis: self.left}
        core = lax.axis_index("core")
        self.to_sib = {"core": 1 - core}
        self.at = lambda place, half: at(place, core, half)
        self.sibling, self.share_own = sibling, share_own
        self.from_sib = []

    def share(self, place, half, source=None):
        if self.sibling:
            target = self.at(place, half)
            source = target if source is None else source
            self.from_sib.append(self.send(source, target, self.to_sib))

    def begin(self):
        def own_to(half, partner):
            return self.send(self.own(half), self.at(self.me, half), partner)

        self.right0 = own_to(0, self.to_right)
        self.left1 = own_to(1, self.to_left)
        self.right1 = own_to(1, self.to_right)
        self.left0 = own_to(0, self.to_left)
        if self.share_own:
            for half in range(2):
                self.share(self.me, half, self.own(half))

    def middle(self):
        self.right0.wait_recv()
        passed = self.at(self.left, 0)
        self.far0 = self.send(passed, passed, self.to_right)
        self.left1.wait_recv()
        passed = self.at(self.right, 1)
        self.far1 = self.send(passed, passed, self.to_left)
        self.share(self.left, 0)
        self.share(self.right, 1)

    def near(self):
        self.right1.wait_recv()
        self.share(self.left, 1)
        self.left0.wait_recv()
        self.share(self.right, 0)

    def end(self):
        self.far0.wait_recv()
        self.share(self.far, 0)
        self.far1.wait_recv()
        self.share(self.far, 1)

    def finish(self):
        for copy in self.from_sib:
            copy.wait_recv()


def run_gathers(gathers):
    for step in ("begin", "middle", "near", "end", "finish"):
        for gather in gathers:
            getattr(gather, step)()


def sems(count):
    return pltpu.SemaphoreType.DMA((count,))


def rows_half(rows):
    return lambda half: (pl.ds(half * rows, rows), slice(None))


def columns_half(columns):
    return lambda half: (slice(None), pl.ds(half * columns, columns))


def weight_gather(send, src, out, half_of):
    core = lax.axis_index("core")
    return RingGather(
        send,
        "dp",
        lambda place, core, half: out.at[(place, core) + half_of(half)],
        lambda half: src.at[(core,) + half_of(half)],
        sibling=True,
    )


def around(axes, sibling=True):
    partners = []
    for axis in axes:
        unused, right, unused, left = ring(axis)
        partners += [{axis: right}, {axis: left}]
    return partners + ([{"core": 1 - lax.axis_index("core")}] if sibling else [])


def start_kernel(hidden, qkv, gains, hidden_out, qkv_out, gains_out, sends, recvs, loads):
    me_x, me_y = lax.axis_index("x"), lax.axis_index("dp")
    far_y = lax.rem(me_y + 2, 4)
    own = [
        pltpu.make_async_copy(hidden, hidden_out.at[:, me_x], loads.at[0]),
        pltpu.make_async_copy(qkv, qkv_out.at[me_y], loads.at[1]),
        pltpu.make_async_copy(gains, gains_out.at[me_y], loads.at[2]),
    ]
    for copy in own:
        copy.start()
    partners = around(["x", "dp"])
    meet(partners + [{"dp": far_y}])
    send = Sends(sends, recvs)
    direct = [
        send(gains, gains_out.at[me_y], partner) for partner in partners[2:4] + [{"dp": far_y}]
    ]
    run_gathers(
        [
            weight_gather(send, qkv, qkv_out, rows_half(64)),
            RingGather(
                send,
                "x",
                lambda place, core, half: hidden_out.at[half, place],
                lambda half: hidden.at[half],
            ),
        ]
    )
    for copy in direct:
        copy.wait_recv()
    for copy in own:
        copy.wait()
    send.finish()


def start_gather(kernel_id, hidden_rows, qkv, gains):
    hidden, qkv, gains = pl.pallas_call(
        start_kernel,
        out_shape=(
            jax.ShapeDtypeStruct((2, 4, BLK, 1024), BF16),
            jax.ShapeDtypeStruct((4, 2, 128, 512), BF16),
            jax.ShapeDtypeStruct((4, 16, 128), BF16),
        ),
        in_specs=[VMEM] * 3,
        out_specs=(ANY,) * 3,
        scratch_shapes=[sems(21), sems(21), sems(3)],
        compiler_params=pltpu.CompilerParams(collective_id=kernel_id, has_side_effects=True),
    )(hidden_rows.reshape(2, BLK, 1024), qkv.reshape(2, 128, 512), gains)
    return hidden.reshape(ROWS, 1024), qkv.reshape(1024, 512), gains


def line_gather_kernel(src, up, out, up_all, sends, recvs, loads):
    own = [
        pltpu.make_async_copy(src, out.at[:, lax.axis_index("x")], loads.at[0]),
        pltpu.make_async_copy(up, up_all.at[lax.axis_index("dp")], loads.at[1]),
    ]
    for copy in own:
        copy.start()
    meet(around(["x", "dp"]))
    send = Sends(sends, recvs)
    run_gathers(
        [
            line_ring(send, src, out),
            weight_gather(send, up, up_all, rows_half(64)),
        ]
    )
    for copy in own:
        copy.wait()
    send.finish()


def line_ring(send, src, out):
    return RingGather(
        send, "x", lambda place, core, half: out.at[half, place], lambda half: src.at[half]
    )


def line_gather(kernel_id, rows, up):
    width = rows.shape[1]
    gathered, up_all = pl.pallas_call(
        line_gather_kernel,
        out_shape=(
            jax.ShapeDtypeStruct((2, 4, BLK, width), BF16),
            jax.ShapeDtypeStruct((4, 2, 128, 1152), BF16),
        ),
        in_specs=[VMEM] * 2,
        out_specs=(ANY,) * 2,
        scratch_shapes=[sems(18), sems(18), sems(2)],
        compiler_params=pltpu.CompilerParams(collective_id=kernel_id, has_side_effects=True),
    )(rows.reshape(2, BLK, width), up.reshape(2, 128, 1152))
    return gathered.reshape(ROWS, width), up_all.reshape(1024, 1152)


def line_gather_pack_kernel(
    src, gate, up, down, out, packed_y, packed_z,
    gu_own, gu_sib, down_own, down_sib, sends, recvs, loads,
):
    core = lax.axis_index("core")
    to_sib = {"core": 1 - core}
    views = [
        (lambda c: gate.at[:, :, c], gu_own.at[0], gu_sib.at[0]),
        (lambda c: up.at[:, :, c], gu_own.at[1], gu_sib.at[1]),
        (lambda c: down.at[:, c], down_own, down_sib),
    ]
    local = [
        pltpu.make_async_copy(view(core), mine, loads.at[i])
        for i, (view, mine, unused) in enumerate(views)
    ]
    local.append(pltpu.make_async_copy(src, out.at[:, lax.axis_index("x")], loads.at[3]))
    for copy in local:
        copy.start()
    meet(around(["x"]))
    send = Sends(sends, recvs)
    line = line_ring(send, src, out)
    line.begin()
    shared = [send(view(1 - core), theirs, to_sib) for view, unused, theirs in views]
    line.middle()
    for copy in local:
        copy.wait()
    for copy in shared:
        copy.wait_recv()

    def pack(y, unused):
        for z in range(4):
            for s in range(2):

                def put(rows, value):
                    if s == 0:
                        packed_y[y, z, rows, :] = value
                    else:
                        packed_z[z, y, rows, :] = value

                for t in range(9):
                    cols = slice(t * 128, (t + 1) * 128)
                    put(
                        slice(t * 32, (t + 1) * 32),
                        add_low(gu_own[s, y, z, :, cols], gu_sib[s, y, z, :, cols]),
                    )
                cols = slice(s * 512 + z * 128, s * 512 + (z + 1) * 128)
                put(slice(288, 432), add_low(down_own[y, :, cols], down_sib[y, :, cols]))
        return unused

    lax.fori_loop(0, 4, pack, 0)
    line.near()
    line.end()
    send.finish()


def line_gather_pack(kernel_id, rows, gate, up, down):
    def vm(*shape):
        return pltpu.VMEM(shape, BF16)

    gathered, packed_y, packed_z = pl.pallas_call(
        line_gather_pack_kernel,
        out_shape=(jax.ShapeDtypeStruct((2, 4, BLK, 1024), BF16),)
        + (jax.ShapeDtypeStruct((4, 4, FF_PIECE, 128), BF16),) * 2,
        in_specs=[VMEM] + [ANY] * 3,
        out_specs=(ANY, VMEM, VMEM),
        scratch_shapes=[
            vm(2, 4, 4, 32, 1152), vm(2, 4, 4, 32, 1152),
            vm(4, 144, 1024), vm(4, 144, 1024),
            sems(9), sems(9), sems(4),
        ],
        compiler_params=pltpu.CompilerParams(
            collective_id=kernel_id, has_side_effects=True, vmem_limit_bytes=40 * 2**20
        ),
    )(
        rows.reshape(2, BLK, 1024),
        gate.reshape(4, 4, 2, 32, 1152),
        up.reshape(4, 4, 2, 32, 1152),
        down.reshape(4, 2, 144, 1024),
    )
    return gathered.reshape(ROWS, 1024), packed_y, packed_z


def sequence_gather_kernel(
    kv, gate, out, kv_all, gate_all, out_all, sends, recvs, loads
):
    me_z, me_y = lax.axis_index("z"), lax.axis_index("dp")
    core = lax.axis_index("core")
    own = [
        pltpu.make_async_copy(kv, kv_all.at[me_z, core], loads.at[0]),
        pltpu.make_async_copy(gate, gate_all.at[me_y], loads.at[1]),
        pltpu.make_async_copy(out, out_all.at[me_y], loads.at[2]),
    ]
    for copy in own:
        copy.start()
    meet(around(["z", "dp"]))
    send = Sends(sends, recvs)
    run_gathers(
        [
            RingGather(
                send,
                "z",
                lambda place, core, half: kv_all.at[place, core, half],
                lambda half: kv.at[half],
                sibling=True,
                share_own=True,
            ),
            weight_gather(send, out, out_all, columns_half(512)),
            weight_gather(send, gate, gate_all, rows_half(64)),
        ]
    )
    for copy in own:
        copy.wait()
    send.finish()


def sequence_gather(kernel_id, kv, gate, out):
    kv_all, gate_all, out_all = pl.pallas_call(
        sequence_gather_kernel,
        out_shape=(
            jax.ShapeDtypeStruct((4, 2, 2, 2 * HD, ROWS), BF16),
            jax.ShapeDtypeStruct((4, 2, 128, 1152), BF16),
            jax.ShapeDtypeStruct((4, 2, 32, 1024), BF16),
        ),
        in_specs=[VMEM] * 3,
        out_specs=(ANY,) * 3,
        scratch_shapes=[sems(38), sems(38), sems(3)],
        compiler_params=pltpu.CompilerParams(collective_id=kernel_id, has_side_effects=True),
    )(kv, gate.reshape(2, 128, 1152), out.reshape(2, 32, 1024))
    return (
        kv_all.reshape(GROUPS, 2, 2 * HD, ROWS),
        gate_all.reshape(1024, 1152),
        out_all.reshape(256, 1024),
    )


def add_low(left, right):
    return (left.astype(F32) + right.astype(F32)).astype(BF16)


def line_scatter_kernel(rider, *refs):
    inputs, outputs = {None: (1, 1), "down": (2, 2), "pieces": (3, 3)}[rider]
    part, *riding = refs[:inputs]
    out, *riding_out = refs[inputs : inputs + outputs]
    pair, self_rows, far_in, left_in, right_in, sends, recvs, loads = refs[inputs + outputs :]
    me, right, far, left = ring("x")
    to_right, to_left = {"x": right}, {"x": left}
    local = [
        pltpu.make_async_copy(part.at[0, right], pair.at[0], loads.at[0]),
        pltpu.make_async_copy(part.at[1, left], pair.at[1], loads.at[1]),
        pltpu.make_async_copy(part.at[0, me], self_rows.at[0], loads.at[2]),
        pltpu.make_async_copy(part.at[1, me], self_rows.at[1], loads.at[3]),
    ]
    for i, (source, target) in enumerate(zip(riding, riding_out)):
        place = lax.axis_index("dp" if rider == "down" else ("z", "x")[i])
        local.append(pltpu.make_async_copy(source, target.at[place], loads.at[4 + i]))
    for copy in local:
        copy.start()
    if rider == "down":
        meet(around(["x", "dp"]))
    else:
        meet(around(["x", "z"] if rider else ["x"], sibling=False))
    send = Sends(sends, recvs)
    far0 = send(part.at[0, far], far_in.at[0], to_right)
    far1 = send(part.at[1, far], far_in.at[1], to_left)
    right1 = send(part.at[1, right], left_in.at[1], to_right)
    left0 = send(part.at[0, left], right_in.at[0], to_left)
    rings = []
    if rider == "down":
        rings = [weight_gather(send, riding[0], riding_out[0], columns_half(512))]
    elif rider == "pieces":
        rows = (pl.ds(0, 224), pl.ds(224, 208))
        rings = [
            RingGather(
                send,
                axis,
                lambda place, core, half, i=i: riding_out[i].at[place, rows[half]],
                lambda half, i=i: riding[i].at[rows[half]],
            )
            for i, axis in enumerate(("z", "x"))
        ]
    for gather in rings:
        gather.begin()
    local[0].wait()
    far0.wait_recv()
    pair[0] = add_low(pair[0], far_in[0])
    right0 = send(pair.at[0], left_in.at[0], to_right)
    local[1].wait()
    far1.wait_recv()
    pair[1] = add_low(pair[1], far_in[1])
    left1 = send(pair.at[1], right_in.at[1], to_left)
    for gather in rings:
        gather.middle()
    for gather in rings:
        gather.near()
    for copy in local[2:]:
        copy.wait()
    right1.wait_recv()
    left0.wait_recv()
    right0.wait_recv()
    left1.wait_recv()
    for h in range(2):
        out[h] = self_rows[h].astype(F32) + left_in[h].astype(F32) + right_in[h].astype(F32)
    for gather in rings:
        gather.end()
    for gather in rings:
        gather.finish()
    send.finish()


def line_scatter(kernel_id, partial, rider=None, riding=()):
    width = partial.shape[1]
    buffer = pltpu.VMEM((2, BLK, width), BF16)
    count = {None: 6, "down": 18, "pieces": 18}[rider]
    gathered = {None: (), "down": ((4, 2, 144, 1024),), "pieces": ((4, FF_PIECE, 128),) * 2}
    result = pl.pallas_call(
        functools.partial(line_scatter_kernel, rider),
        out_shape=(jax.ShapeDtypeStruct((2, BLK, width), F32),)
        + tuple(jax.ShapeDtypeStruct(shape, BF16) for shape in gathered[rider]),
        in_specs=[ANY] + [VMEM] * len(riding),
        out_specs=(VMEM,) + (ANY,) * len(riding),
        scratch_shapes=[buffer] * 5 + [sems(count), sems(count), sems(6)],
        compiler_params=pltpu.CompilerParams(
            collective_id=kernel_id, has_side_effects=True, vmem_limit_bytes=32 * 2**20
        ),
    )(partial.reshape(2, 4, BLK, width), *riding)
    summed = result[0].reshape(2 * BLK, width)
    return (summed, *result[1:]) if rider else summed


class RingSum:
    def __init__(self, send, axis, chunk, far_in, left_in, right_in):
        self.send, self.chunk = send, chunk
        self.far_in, self.left_in, self.right_in = far_in, left_in, right_in
        self.me, self.right, self.far, self.left = ring(axis)
        self.to_right, self.to_left = {axis: self.right}, {axis: self.left}

    def begin(self):
        send, chunk = self.send, self.chunk
        self.far0 = send(chunk(self.far, 0), self.far_in(0), self.to_right)
        self.far1 = send(chunk(self.far, 1), self.far_in(1), self.to_left)
        self.right1 = send(chunk(self.right, 1), self.left_in(1), self.to_right)
        self.left0 = send(chunk(self.left, 0), self.right_in(0), self.to_left)

    def middle(self):
        send, chunk = self.send, self.chunk
        self.far0.wait_recv()
        mine = chunk(self.right, 0)
        mine[...] = add_low(mine[...], self.far_in(0)[...])
        self.right0 = send(mine, self.left_in(0), self.to_right)
        self.far1.wait_recv()
        mine = chunk(self.left, 1)
        mine[...] = add_low(mine[...], self.far_in(1)[...])
        self.left1 = send(mine, self.right_in(1), self.to_left)

    def end(self, store):
        self.right1.wait_recv()
        self.left0.wait_recv()
        self.right0.wait_recv()
        self.left1.wait_recv()
        for h in range(2):
            store(
                h,
                self.chunk(self.me, h)[...].astype(F32)
                + self.left_in(h)[...].astype(F32)
                + self.right_in(h)[...].astype(F32),
            )


class PieceSums:
    def __init__(
        self, send, packed, far_a, left_a, right_a, mid, far_b, left_b, right_b, rows, order
    ):
        self.send, self.mid = send, mid
        two = (pl.ds(0, 2), pl.ds(2, 2))
        chunks = (
            lambda place, h: packed.at[0, place, two[h]],
            lambda place, h: packed.at[(1, two[h], place) if order else (1, place, two[h])],
        )
        self.first = [
            RingSum(
                send,
                axis,
                chunks[s],
                lambda h, s=s: far_a.at[s, h],
                lambda h, s=s: left_a.at[s, h],
                lambda h, s=s: right_a.at[s, h],
            )
            for s, axis in enumerate(("dp", "z"))
        ]
        self.second = [
            RingSum(
                send,
                axis,
                lambda place, h, s=s: mid.at[s, place, rows[h]],
                lambda h, s=s: far_b.at[s, rows[h]],
                lambda h, s=s: left_b.at[s, rows[h]],
                lambda h, s=s: right_b.at[s, rows[h]],
            )
            for s, axis in enumerate(("z", "dp"))
        ]

    def begin(self):
        for step in self.first:
            step.begin()

    def middle(self):
        for step in self.first:
            step.middle()

    def turn(self):
        for s in range(2):

            def keep(h, value, s=s):
                self.mid[s, 2 * h : 2 * h + 2] = value.astype(BF16)

            self.first[s].end(keep)
            self.second[s].begin()

    def late(self):
        for step in self.second:
            step.middle()

    def end(self, keep):
        for s in range(2):
            self.second[s].end(functools.partial(keep, s))


def piece_buffers(rows):
    def vm(*shape):
        return pltpu.VMEM(shape, BF16)

    return (
        [vm(2, 4, 4, rows, 128)]
        + [vm(2, 2, 2, rows, 128)] * 3
        + [vm(2, 4, rows, 128)]
        + [vm(2, rows, 128)] * 3
    )


def attend_back_kernel(
    q_ref, kv_ref, qo_ref, ko_ref, mixed_ref, log_ref, grad_ref, packed_y, packed_z,
    dq_ref, dkv_ref, piece_ref,
    dkv_acc, packed, far_a, left_a, right_a, mid, far_b, left_b, right_b, sends, recvs, loads,
):
    local = [
        pltpu.make_async_copy(source, packed.at[i], loads.at[i])
        for i, source in enumerate((packed_y, packed_z))
    ]
    for copy in local:
        copy.start()
    meet(around(["dp", "z"], sibling=False))
    for copy in local:
        copy.wait()
    shares = (pl.ds(0, 224), pl.ds(224, 208))
    sums = PieceSums(
        Sends(sends, recvs), packed, far_a, left_a, right_a, mid, far_b, left_b, right_b, shares, 0
    )
    sums.begin()

    dkv_acc[...] = jnp.zeros_like(dkv_acc)
    for half in range(2):
        cols = slice(half * HALF, (half + 1) * HALF)
        q_order = jnp.concatenate([qo_ref[:, cols]] * 2, axis=1)
        queries = [head_pair(q_ref, kv_head, cols) for kv_head in range(2)]
        grads = [head_pair(grad_ref, kv_head, cols) for kv_head in range(2)]
        logs = [
            jnp.concatenate([log_ref[at : at + 1, cols], log_ref[at + 1 : at + 2, cols]], axis=1)
            for at in (0, 2)
        ]
        dots = [
            jnp.sum(
                head_pair(mixed_ref, kv_head, cols) * grads[kv_head].astype(F32),
                axis=0,
                keepdims=True,
            )
            for kv_head in range(2)
        ]

        def group(g, carried):
            carried = list(carried)
            for k_half in range(half + 1):
                keys = slice(k_half * HALF, (k_half + 1) * HALF)
                for kv_head in range(2):
                    q_t, grad_t = queries[kv_head], grads[kv_head]
                    k_t = kv_ref[g, kv_head, 0:HD, keys]
                    v_t = kv_ref[g, kv_head, HD : 2 * HD, keys]
                    probs = jnp.exp2(scores_of(k_t, q_t) * EXP2_SCALE - logs[kv_head])
                    if k_half == half:
                        allowed = ko_ref[g, keys, :] <= q_order
                        probs = jnp.where(allowed, probs, 0.0)
                    score_grad = (probs * (scores_of(v_t, grad_t) - dots[kv_head])).astype(BF16)
                    dkv_acc[g, kv_head, HD : 2 * HD, keys] += dot(
                        grad_t, probs.astype(BF16), 1, 1
                    )
                    dkv_acc[g, kv_head, 0:HD, keys] += dot(q_t, score_grad, 1, 1)
                    carried[kv_head] = carried[kv_head] + dot(k_t, score_grad)
            return tuple(carried)

        start = jnp.zeros((HD, 2 * HALF), F32)
        if half == 0:
            query_grads = lax.fori_loop(0, GROUPS, group, (start, start))
            sums.middle()
        else:
            query_grads = lax.fori_loop(0, GROUPS // 2, group, (start, start))
            sums.turn()
            query_grads = lax.fori_loop(GROUPS // 2, GROUPS, group, query_grads)
        for kv_head, dq in enumerate(query_grads):
            for head in range(2):
                at = 2 * kv_head + head
                rows = slice(at * HD, (at + 1) * HD)
                dq_ref[rows, cols] = dq[:, head * HALF : (head + 1) * HALF] * SCORE_SCALE

    def finish(g, unused):
        for kv_head in range(2):
            dkv_ref[g, kv_head, 0:HD, :] = (dkv_acc[g, kv_head, 0:HD, :] * SCORE_SCALE).astype(
                BF16
            )
            dkv_ref[g, kv_head, HD : 2 * HD, :] = dkv_acc[g, kv_head, HD : 2 * HD, :].astype(BF16)
        return unused

    sums.late()
    lax.fori_loop(0, GROUPS, finish, 0)

    def keep(s, half, value):
        piece_ref[s, shares[half], :] = value.astype(BF16)

    sums.end(keep)
    sums.send.finish()


def attend_back(kernel_id, q_t, kv_all, q_order, k_order, mixed, log_total, mixed_grad, packed):
    return pl.pallas_call(
        attend_back_kernel,
        out_shape=(
            jax.ShapeDtypeStruct((4 * HD, ROWS), F32),
            jax.ShapeDtypeStruct((GROUPS, 2, 2 * HD, ROWS), BF16),
            jax.ShapeDtypeStruct((2, FF_PIECE, 128), BF16),
        ),
        in_specs=[VMEM] * 7 + [ANY] * 2,
        out_specs=(VMEM,) * 3,
        scratch_shapes=[pltpu.VMEM((GROUPS, 2, 2 * HD, ROWS), F32)]
        + piece_buffers(FF_PIECE)
        + [sems(24), sems(24), sems(2)],
        compiler_params=pltpu.CompilerParams(
            collective_id=kernel_id, has_side_effects=True, vmem_limit_bytes=48 * 2**20
        ),
    )(q_t, kv_all, q_order, k_order, mixed, log_total, mixed_grad, *packed)


def sequence_scatter_kernel(
    part, out, own, other, far_in, left_in, right_in, sends, recvs, loads
):
    core = lax.axis_index("core")
    me, right, far, left = ring("z")
    order = (far, right, left, me)
    local = [
        pltpu.make_async_copy(part.at[place, core], own.at[place], loads.at[i])
        for i, place in enumerate(order)
    ]
    for copy in local:
        copy.start()
    to_sib = {"core": 1 - core}
    meet([{"z": right}, {"z": left}, to_sib])
    send = Sends(sends, recvs)
    shared = [send(part.at[place, 1 - core], other.at[place], to_sib) for place in order]

    def merge(i):
        local[i].wait()
        shared[i].wait_recv()
        own[order[i]] = add_low(own[order[i]], other[order[i]])

    ring_sum = RingSum(
        send,
        "z",
        lambda place, h: own.at[place, h],
        lambda h: far_in.at[h],
        lambda h: left_in.at[h],
        lambda h: right_in.at[h],
    )
    for i in range(3):
        merge(i)
    ring_sum.begin()
    merge(3)
    ring_sum.middle()

    def store(h, value):
        out[h] = value

    ring_sum.end(store)
    send.finish()


def sequence_scatter(kernel_id, partial):
    buffer = pltpu.VMEM((2, 2 * HD, ROWS), BF16)
    wide = pltpu.VMEM((4, 2, 2 * HD, ROWS), BF16)
    return pl.pallas_call(
        sequence_scatter_kernel,
        out_shape=jax.ShapeDtypeStruct((2, 2 * HD, ROWS), F32),
        in_specs=[ANY],
        out_specs=VMEM,
        scratch_shapes=[wide, wide, buffer, buffer, buffer]
        + [
            pltpu.SemaphoreType.DMA((10,)),
            pltpu.SemaphoreType.DMA((10,)),
            pltpu.SemaphoreType.DMA((4,)),
        ],
        compiler_params=pltpu.CompilerParams(
            collective_id=kernel_id, has_side_effects=True, vmem_limit_bytes=32 * 2**20
        ),
    )(partial.reshape(4, 2, 2, 2 * HD, ROWS))


def grads_kernel(
    qkv, out, gains, ff_a, ff_b, result, gain_sums, ff_out,
    qkv_own, qkv_sib, out_own, out_sib, gain_slots,
    packed, far_a, left_a, right_a, mid, far_b, left_b, right_b,
    sends, recvs, loads,
):
    core = lax.axis_index("core")
    to_sib = {"core": 1 - core}
    views = [
        (lambda c: qkv.at[:, :, c], qkv_own, qkv_sib),
        (lambda c: out.at[:, c], out_own, out_sib),
    ]
    local = [
        pltpu.make_async_copy(view(core), mine, loads.at[i])
        for i, (view, mine, unused) in enumerate(views)
    ]
    local += [
        pltpu.make_async_copy(
            ff_a, ff_out.at[0, core, :, lax.axis_index("x")], loads.at[2]
        ),
        pltpu.make_async_copy(ff_b, ff_out.at[1, core, lax.axis_index("z")], loads.at[3]),
    ]
    for copy in local:
        copy.start()
    peers = {axis: [{axis: place} for place in ring(axis)[1:]] for axis in ("z", "dp", "x")}
    meet(peers["z"] + peers["dp"] + peers["x"] + [to_sib])
    send = Sends(sends, recvs)

    def gain_begin(step, axis, value):
        place = lax.axis_index(axis)
        gain_slots[step, place] = value
        slot = gain_slots.at[step, place]
        return [send(slot, slot, to) for to in ([to_sib] if axis == "core" else peers[axis])]

    def gain_end(step, copies):
        for copy in copies:
            copy.wait_recv()
        total = gain_slots[step, 0] + gain_slots[step, 1]
        for place in range(2, 4 if step else 2):
            total = total + gain_slots[step, place]
        return total

    gain_copies = gain_begin(0, "core", gains[...])
    shared = [send(view(1 - core), theirs, to_sib) for view, unused, theirs in views]
    two = (pl.ds(0, 2), pl.ds(2, 2))
    bulk = [
        RingGather(
            send,
            "x",
            lambda place, core, half: ff_out.at[0, core, two[half], place],
            lambda half: ff_a.at[two[half]],
            sibling=True,
            share_own=True,
        ),
        RingGather(
            send,
            "z",
            lambda place, core, half: ff_out.at[1, core, place, two[half]],
            lambda half: ff_b.at[two[half]],
            sibling=True,
            share_own=True,
        ),
    ]
    for gather in bulk:
        gather.begin()
    for copy in local:
        copy.wait()
    for copy in shared:
        copy.wait_recv()

    def pack(y, unused):
        for z in range(4):
            for s in range(2):
                for t in range(2):
                    cols = slice(s * 256 + t * 128, s * 256 + (t + 1) * 128)
                    packed[s, y, z, t * 32 : (t + 1) * 32, :] = add_low(
                        qkv_own[y, z, :, cols], qkv_sib[y, z, :, cols]
                    )
                cols = slice(s * 512 + z * 128, s * 512 + (z + 1) * 128)
                packed[s, y, z, 64:96, :] = add_low(out_own[y, :, cols], out_sib[y, :, cols])
        return unused

    lax.fori_loop(0, 4, pack, 0)
    rows = (pl.ds(0, 48), pl.ds(48, 48))
    sums = PieceSums(
        send, packed, far_a, left_a, right_a, mid, far_b, left_b, right_b, rows, 1
    )
    sums.begin()
    gain_copies = gain_begin(1, "z", gain_end(0, gain_copies))
    sums.middle()
    for gather in bulk:
        gather.middle()
    gain_copies = gain_begin(2, "dp", gain_end(1, gain_copies))
    sums.turn()
    gain_copies = gain_begin(3, "x", gain_end(2, gain_copies))
    for gather in bulk:
        gather.near()
    sums.late()

    def keep(s, half, value):
        result[s, rows[half], :] = value.astype(BF16)

    sums.end(keep)
    gain_sums[...] = gain_end(3, gain_copies)
    for gather in bulk:
        gather.end()
    for gather in bulk:
        gather.finish()
    send.finish()


def sum_grads(kernel_id, qkv, out, gains, ff_a, ff_b):
    def vm(*shape):
        return pltpu.VMEM(shape, BF16)

    return pl.pallas_call(
        grads_kernel,
        out_shape=(
            jax.ShapeDtypeStruct((2, PIECE, 128), BF16),
            jax.ShapeDtypeStruct((24, 128), F32),
            jax.ShapeDtypeStruct((2, 2, 4, 4, FF_PIECE, 128), BF16),
        ),
        in_specs=[ANY] * 2 + [VMEM] * 3,
        out_specs=(VMEM, VMEM, ANY),
        scratch_shapes=[
            vm(4, 4, 32, 512), vm(4, 4, 32, 512),
            vm(4, 32, 1024), vm(4, 32, 1024),
            pltpu.VMEM((4, 4, 24, 128), F32),
        ]
        + piece_buffers(PIECE)
        + [sems(64), sems(64), sems(4)],
        compiler_params=pltpu.CompilerParams(
            collective_id=kernel_id, has_side_effects=True, vmem_limit_bytes=48 * 2**20
        ),
    )(qkv.reshape(4, 4, 2, 32, 512), out.reshape(4, 2, 32, 1024), gains, ff_a, ff_b)


class RingCopy:
    def __init__(self, send, axis, place_of):
        self.send, self.at = send, place_of
        self.me, self.right, self.far, self.left = ring(axis)
        self.to_right, self.to_left = {axis: self.right}, {axis: self.left}

    def begin(self):
        me = self.me
        self.right0 = self.send(self.at(me, 0), self.at(me, 0), self.to_right)
        self.left1 = self.send(self.at(me, 1), self.at(me, 1), self.to_left)
        self.right1 = self.send(self.at(me, 1), self.at(me, 1), self.to_right)
        self.left0 = self.send(self.at(me, 0), self.at(me, 0), self.to_left)

    def middle(self):
        self.right0.wait_recv()
        self.far0 = self.send(self.at(self.left, 0), self.at(self.left, 0), self.to_right)
        self.left1.wait_recv()
        self.far1 = self.send(self.at(self.right, 1), self.at(self.right, 1), self.to_left)

    def near(self):
        self.right1.wait_recv()
        self.left0.wait_recv()

    def end(self):
        self.far0.wait_recv()
        self.far1.wait_recv()


def spread_kernel(piece, out, sends, recvs, loads):
    core = lax.axis_index("core")
    me_x, me_z = lax.axis_index("x"), lax.axis_index("z")
    to_sib = {"core": 1 - core}
    own = [
        pltpu.make_async_copy(piece.at[s], out.at[s, core, me_z, me_x], loads.at[s])
        for s in range(2)
    ]
    for copy in own:
        copy.start()
    meet(around(["x", "z"]))
    send = Sends(sends, recvs)
    rows = (pl.ds(0, 48), pl.ds(48, 48))
    two = (pl.ds(0, 2), pl.ds(2, 2))
    first = [
        RingCopy(send, "z", lambda place, h: out.at[0, core, place, me_x, rows[h]]),
        RingCopy(send, "x", lambda place, h: out.at[1, core, me_z, place, rows[h]]),
    ]
    second = [
        RingCopy(send, "x", lambda place, h: out.at[0, core, two[h], place]),
        RingCopy(send, "z", lambda place, h: out.at[1, core, place, two[h]]),
    ]
    shared = []

    def share(s, place):
        view = out.at[0, core, :, place] if s == 0 else out.at[1, core, place]
        shared.append(send(view, view, to_sib))

    for copy in own:
        copy.wait()
    for step in first:
        step.begin()
    for step in first:
        step.middle()
    for s in range(2):
        first[s].near()
        first[s].end()
        second[s].begin()
        share(s, second[s].me)
    for step in second:
        step.middle()
    for s in range(2):
        second[s].near()
        share(s, second[s].left)
        share(s, second[s].right)
    for s in range(2):
        second[s].end()
        share(s, second[s].far)
    for copy in shared:
        copy.wait_recv()
    send.finish()


def spread(kernel_id, piece):
    return pl.pallas_call(
        spread_kernel,
        out_shape=jax.ShapeDtypeStruct((2, 2, 4, 4, PIECE, 128), BF16),
        in_specs=[VMEM],
        out_specs=ANY,
        scratch_shapes=[sems(32), sems(32), sems(2)],
        compiler_params=pltpu.CompilerParams(collective_id=kernel_id, has_side_effects=True),
    )(piece)


def unpack_rows_kernel(ff_pieces, pieces, gate, up, query, key, value):
    for x in range(4):
        for t in range(9):
            cols = slice(x * 1152 + t * 128, x * 1152 + (t + 1) * 128)
            gate[:, cols] = ff_pieces[0, 0, 0, x, t * 32 : (t + 1) * 32, :].astype(F32)
            up[:, cols] = ff_pieces[1, 0, 0, x, t * 32 : (t + 1) * 32, :].astype(F32)
        for t in range(2):
            cols = slice(x * 256 + t * 128, x * 256 + (t + 1) * 128)
            query[:, cols] = pieces[0, 0, 0, x, t * 32 : (t + 1) * 32, :].astype(F32)
        cols = slice(x * 128, (x + 1) * 128)
        key[:, cols] = pieces[1, 0, 0, x, 0:32, :].astype(F32)
        value[:, cols] = pieces[1, 0, 0, x, 32:64, :].astype(F32)


def unpack_columns_kernel(ff_pieces, pieces, down, out):
    for s in range(2):
        for z in range(4):
            cols = slice(s * 512 + z * 128, s * 512 + (z + 1) * 128)
            down[:, cols] = ff_pieces[s, 0, z, 0].astype(F32)
            out[:, cols] = pieces[s, 0, z, 0].astype(F32)


def unpack(ff_pieces, pieces):
    rows = pl.pallas_call(
        unpack_rows_kernel,
        grid=(4, 2),
        out_shape=tuple(
            jax.ShapeDtypeStruct((256, width), F32) for width in (4608, 4608, 1024, 512, 512)
        ),
        in_specs=[
            pl.BlockSpec((2, 1, 1, 4, 288, 128), lambda z, c: (0, c, z, 0, 0, 0)),
            pl.BlockSpec((2, 1, 1, 4, PIECE, 128), lambda z, c: (0, c, z, 0, 0, 0)),
        ],
        out_specs=tuple(
            pl.BlockSpec((32, width), lambda z, c: (2 * z + c, 0))
            for width in (4608, 4608, 1024, 512, 512)
        ),
        compiler_params=pltpu.CompilerParams(vmem_limit_bytes=32 * 2**20),
    )(ff_pieces, pieces)
    columns = pl.pallas_call(
        unpack_columns_kernel,
        grid=(4, 2),
        out_shape=(
            jax.ShapeDtypeStruct((1152, 1024), F32),
            jax.ShapeDtypeStruct((256, 1024), F32),
        ),
        in_specs=[
            pl.BlockSpec((2, 1, 4, 1, 144, 128), lambda x, c: (0, c, 0, x, 2, 0)),
            pl.BlockSpec((2, 1, 4, 1, 32, 128), lambda x, c: (0, c, 0, x, 2, 0)),
        ],
        out_specs=(
            pl.BlockSpec((144, 1024), lambda x, c: (2 * x + c, 0)),
            pl.BlockSpec((32, 1024), lambda x, c: (2 * x + c, 0)),
        ),
        compiler_params=pltpu.CompilerParams(vmem_limit_bytes=32 * 2**20),
    )(ff_pieces, pieces)
    return rows + columns


def after(value, anchor):
    return lax.optimization_barrier((value, anchor))[0]


SWAP = [(a * 4 + b, b * 4 + a) for a in range(4) for b in range(4)]


def on_device(
    hidden_in,
    positions,
    block_of,
    attn_gain,
    query_weight,
    key_weight,
    value_weight,
    out_weight,
    query_gain,
    key_gain,
    ffn_gain,
    gate_weight,
    up_weight,
    down_weight,
    cotangent,
):
    z_at = lax.axis_index("z")
    x_at = lax.axis_index("x")
    core_at = lax.axis_index("core")
    dp_at = lax.axis_index("dp")

    hidden_rows = hidden_in[0]
    grad_rows = cotangent[0]

    in_block = jnp.arange(BLK, dtype=jnp.int32)
    blocks = block_of.reshape(4, 4, 2, 2).transpose(0, 2, 3, 1)
    order_all = (blocks[..., None] * BLK + in_block).reshape(GROUPS, ROWS)
    own_order = lax.dynamic_index_in_dim(order_all, z_at * 2 + core_at, 0, keepdims=True)
    k_order = order_all.reshape(GROUPS, ROWS, 1)
    own_slot = 2 * (z_at * 8 + x_at * 2 + core_at)
    first_block = lax.dynamic_index_in_dim(block_of, own_slot, 0, keepdims=False)
    offset = positions[0, 0] - first_block * BLK
    frequency = ROPE_BASE ** (-2.0 * jnp.arange(HD // 2, dtype=F32) / HD)
    angles = (own_order + offset).astype(F32) * frequency[:, None]
    cosine, sine = jnp.cos(angles), jnp.sin(angles)

    def columns(weight, width):
        return lax.dynamic_slice_in_dim(weight, x_at * width, width, axis=1)

    def swapped_rows(weight, rows):
        own = lax.dynamic_slice_in_dim(weight, x_at * rows, rows, axis=0)
        return lax.ppermute(own, ("dp", "x"), SWAP)

    gains_own = jnp.pad(
        jnp.concatenate([attn_gain, ffn_gain, query_gain, key_gain]), (0, 2048 - 544)
    )
    qkv_own = jnp.concatenate(
        [columns(query_weight, 256), columns(key_weight, 128), columns(value_weight, 128)],
        axis=1,
    )

    hidden = hidden_rows.astype(F32)
    line_hidden, qkv_weight, gains = start_gather(
        0, hidden_rows, qkv_own, gains_own.reshape(16, 128)
    )
    gains = gains.reshape(4, 2048).astype(F32)
    attn_gain_all = gains[:, 0:256].reshape(1024)
    ffn_gain_all = gains[:, 256:512].reshape(1024)
    query_gain_all = gains[:, 512:528].reshape(HD)
    key_gain_all = gains[:, 528:544].reshape(HD)
    out_own = swapped_rows(after(out_weight, line_hidden), 64)
    down_own = swapped_rows(after(down_weight, line_hidden), 288)
    branch_low = lax.all_gather(after(grad_rows, line_hidden).reshape(2, BLK, 1024), "x", axis=1).reshape(ROWS, 1024)
    attn_in = rms_scale(line_hidden.astype(F32), attn_gain_all).astype(BF16)
    qkv_t = dot(qkv_weight, attn_in, 0, 1)
    q_rot, q_back = jax.vjp(
        lambda r, g: head_norm_rope(r, g, cosine, sine),
        qkv_t[0:256].reshape(4, HD, ROWS),
        query_gain_all,
    )
    k_rot, k_back = jax.vjp(
        lambda r, g: head_norm_rope(r, g, cosine, sine),
        qkv_t[256:384].reshape(2, HD, ROWS),
        key_gain_all,
    )
    q_low = q_rot.reshape(4 * HD, ROWS).astype(BF16)
    kv_low = jnp.concatenate([k_rot, qkv_t[384:512].reshape(2, HD, ROWS)], axis=1).astype(BF16)
    kv_all, gate_slice, out_slice = sequence_gather(
        1, kv_low, columns(gate_weight, 1152), out_own
    )
    mixed, attn_low, log_total = attend(q_low, kv_all, own_order, k_order)
    attn_rows, down_slice = line_scatter(
        2, dot(attn_low, out_slice, 0, 0).astype(BF16), "down", (down_own.reshape(2, 144, 1024),)
    )
    down_slice = down_slice.reshape(1152, 1024)
    after_attn = hidden + attn_rows
    normed_ffn, norm_ffn_back = jax.vjp(rms_scale, after_attn, ffn_gain_all)
    ffn_in, up_slice = line_gather(3, normed_ffn.astype(BF16), columns(up_weight, 1152))
    gate_proj = dot(ffn_in, gate_slice)
    up_proj = dot(ffn_in, up_slice)
    activated, swiglu_back = jax.vjp(lambda g, u: jax.nn.silu(g) * u, gate_proj, up_proj)
    activated_low = activated.astype(BF16)
    residual_grad = grad_rows.astype(F32)
    activated_grad = dot(branch_low, down_slice, 1, 1)
    gate_grad, up_grad = swiglu_back(activated_grad)
    gate_grad_low = gate_grad.astype(BF16)
    up_grad_low = up_grad.astype(BF16)
    ffn_in_grad = line_scatter(
        5,
        (dot(gate_grad_low, gate_slice, 1, 1) + dot(up_grad_low, up_slice, 1, 1)).astype(BF16),
    )
    mid_part, ffn_gain_part = norm_ffn_back(ffn_in_grad)
    mid_grad = residual_grad + mid_part
    branch_attn, packed_y, packed_z = line_gather_pack(
        6,
        mid_grad.astype(BF16),
        dot(ffn_in, gate_grad_low, 0, 0).astype(BF16),
        dot(ffn_in, up_grad_low, 0, 0).astype(BF16),
        dot(activated_low, branch_low, 0, 0).astype(BF16),
    )
    branch_attn, late_activated = lax.optimization_barrier((branch_attn, activated_low))
    out_part = dot(late_activated, down_slice).astype(BF16).reshape(2, 4, BLK, 1024)
    branch_attn, out_part = lax.optimization_barrier((branch_attn, out_part))
    layer_out = (
        after_attn
        + lax.psum_scatter(
            out_part.transpose(1, 0, 2, 3).reshape(ROWS, 1024),
            "x",
            scatter_dimension=0,
            tiled=True,
        ).astype(F32)
    ).astype(BF16)

    mixed_grad = dot(out_slice, branch_attn, 1, 1).astype(BF16)
    q_grad, kv_grad_all, ff_piece = attend_back(
        11, q_low, kv_all, own_order, k_order, mixed, log_total, mixed_grad, (packed_y, packed_z)
    )
    ff_swapped = lax.ppermute(ff_piece[:, 288:], ("dp", "x"), SWAP)
    ff_piece = jnp.concatenate([ff_piece[:, :288], ff_swapped], axis=1)
    kv_grad = sequence_scatter(7, kv_grad_all)
    q_pre, q_gain_part = q_back(q_grad.reshape(4, HD, ROWS))
    k_pre, k_gain_part = k_back(kv_grad[:, 0:HD])
    qkv_pre = jnp.concatenate(
        [
            q_pre.reshape(4 * HD, ROWS),
            k_pre.reshape(2 * HD, ROWS),
            kv_grad[:, HD:].reshape(2 * HD, ROWS),
        ],
        axis=0,
    ).astype(BF16)
    attn_in_grad, ff_a, ff_b = line_scatter(
        8,
        dot(qkv_pre, qkv_weight, 0, 1).astype(BF16),
        "pieces",
        (ff_piece[0], ff_piece[1]),
    )
    unused, norm_attn_back = jax.vjp(rms_scale, hidden, attn_gain_all)
    hidden_part, attn_gain_part = norm_attn_back(attn_in_grad)
    input_grad = (mid_grad + hidden_part).astype(BF16)

    gain_parts = jnp.concatenate([attn_gain_part, ffn_gain_part, q_gain_part, k_gain_part])
    gain_parts = jnp.pad(gain_parts, (0, 3072 - 2176)).reshape(24, 128)

    def own_slice(begin, size):
        return lax.dynamic_slice_in_dim(
            gain_sums[begin : begin + size], dp_at * (size // 4), size // 4
        )

    own_piece, gain_sums, ff_pieces = sum_grads(
        9,
        dot(attn_in, qkv_pre, 0, 1).astype(BF16),
        dot(attn_low, branch_attn).astype(BF16),
        gain_parts,
        ff_a,
        ff_b,
    )
    gain_sums = gain_sums.reshape(3072)
    swapped = lax.ppermute(own_piece[:, 64:], ("dp", "x"), SWAP)
    pieces = spread(10, jnp.concatenate([own_piece[:, :64], swapped], axis=1))
    gate_all, up_all, query_all, key_all, value_all, down_all, out_all = unpack(ff_pieces, pieces)
    return (
        layer_out[None],
        input_grad[None],
        own_slice(0, 1024),
        query_all,
        key_all,
        value_all,
        out_all,
        own_slice(2048, 64),
        own_slice(2112, 64),
        own_slice(1024, 1024),
        gate_all,
        up_all,
        down_all,
    )


def solution(mesh):
    fine = Mesh(mesh.devices.reshape(4, 4, 4, 2), ("dp", "z", "x", "core"))
    ctx = ("z", "x", "core")
    rows = P("dp", ctx, None)
    vector, matrix = P("dp"), P("dp", None)
    return jax.shard_map(
        on_device,
        mesh=fine,
        in_specs=(rows, P("dp", ctx), P(), vector)
        + (matrix,) * 4
        + (vector,) * 3
        + (matrix,) * 3
        + (rows,),
        out_specs=(rows, rows, vector) + (matrix,) * 4 + (vector,) * 3 + (matrix,) * 3,
        check_vma=False,
    )
```

```python
import functools

import jax
import jax.numpy as jnp
import numpy as np
from jax import lax
from jax.experimental import pallas as pl
from jax.experimental.pallas import tpu as pltpu
from jax.sharding import Mesh, PartitionSpec as P

HD = 64
BLK = 64
GROUPS = 8
HALF = 256
ROWS = 512
FF_PIECE = 432

NORM_EPS = 1e-05
ROPE_BASE = 1000000.0
EXP2_SCALE = float(HD**-0.5 * np.log2(np.e))
SCORE_SCALE = HD**-0.5

F32 = jnp.float32
BF16 = jnp.bfloat16
VMEM = pl.BlockSpec(memory_space=pltpu.VMEM)
ANY = pl.BlockSpec(memory_space=pl.ANY)


def dot(left, right, left_dim=1, right_dim=0):
    return lax.dot_general(
        left, right, (((left_dim,), (right_dim,)), ((), ())), preferred_element_type=F32
    )


def rms_scale(values, gain):
    return values * lax.rsqrt(jnp.mean(values * values, axis=-1, keepdims=True) + NORM_EPS) * gain


def head_norm_rope(raw, gain, cosine, sine):
    scaled = (
        raw
        * lax.rsqrt(jnp.mean(raw * raw, axis=1, keepdims=True) + NORM_EPS)
        * gain[None, :, None]
    )
    front = scaled[:, : HD // 2]
    back = scaled[:, HD // 2 :]
    return jnp.concatenate([front * cosine - back * sine, back * cosine + front * sine], axis=1)


def scores_of(keys_t, queries_t):
    return dot(keys_t, queries_t, 0, 0)


def head_pair(ref, kv_head, cols):
    first = 2 * kv_head * HD
    return jnp.concatenate(
        [ref[first : first + HD, cols], ref[first + HD : first + 2 * HD, cols]], axis=1
    )


def ring(axis):
    me = lax.axis_index(axis)
    return me, lax.rem(me + 1, 4), lax.rem(me + 2, 4), lax.rem(me + 3, 4)


def meet(partners):
    barrier = pltpu.get_barrier_semaphore()
    for partner in partners:
        pl.semaphore_signal(
            barrier, inc=1, device_id=partner, device_id_type=pl.DeviceIdType.MESH
        )
    pl.semaphore_wait(barrier, len(partners))


class Sends:
    def __init__(self, send_sems, recv_sems):
        self.send_sems, self.recv_sems, self.started = send_sems, recv_sems, []

    def __call__(self, source, target, partner):
        at = len(self.started)
        copy = pltpu.make_async_remote_copy(
            src_ref=source,
            dst_ref=target,
            send_sem=self.send_sems.at[at],
            recv_sem=self.recv_sems.at[at],
            device_id=partner,
            device_id_type=pl.DeviceIdType.MESH,
        )
        copy.start()
        self.started.append(copy)
        return copy

    def finish(self):
        for copy in self.started:
            copy.wait_send()


class RingGather:
    def __init__(self, send, axis, at, own, sibling=False, share_own=False):
        self.send, self.axis, self.own = send, axis, own
        self.me, self.right, self.far, self.left = ring(axis)
        self.to_right, self.to_left = {axis: self.right}, {axis: self.left}
        core = lax.axis_index("core")
        self.to_sib = {"core": 1 - core}
        self.at = lambda place, half: at(place, core, half)
        self.sibling, self.share_own = sibling, share_own
        self.from_sib = []

    def share(self, place, half, source=None):
        if self.sibling:
            target = self.at(place, half)
            source = target if source is None else source
            self.from_sib.append(self.send(source, target, self.to_sib))

    def begin(self):
        def own_to(half, partner):
            return self.send(self.own(half), self.at(self.me, half), partner)

        self.right0 = own_to(0, self.to_right)
        self.left1 = own_to(1, self.to_left)
        self.right1 = own_to(1, self.to_right)
        self.left0 = own_to(0, self.to_left)
        if self.share_own:
            for half in range(2):
                self.share(self.me, half, self.own(half))

    def middle(self):
        self.right0.wait_recv()
        passed = self.at(self.left, 0)
        self.far0 = self.send(passed, passed, self.to_right)
        self.left1.wait_recv()
        passed = self.at(self.right, 1)
        self.far1 = self.send(passed, passed, self.to_left)
        self.share(self.left, 0)
        self.share(self.right, 1)

    def near(self):
        self.right1.wait_recv()
        self.share(self.left, 1)
        self.left0.wait_recv()
        self.share(self.right, 0)

    def end(self):
        self.far0.wait_recv()
        self.share(self.far, 0)
        self.far1.wait_recv()
        self.share(self.far, 1)

    def finish(self):
        for copy in self.from_sib:
            copy.wait_recv()


def sems(count):
    return pltpu.SemaphoreType.DMA((count,))


def rows_half(rows):
    return lambda half: (pl.ds(half * rows, rows), slice(None))


def columns_half(columns):
    return lambda half: (slice(None), pl.ds(half * columns, columns))


def weight_gather(send, src, out, half_of):
    core = lax.axis_index("core")
    return RingGather(
        send,
        "dp",
        lambda place, core, half: out.at[(place, core) + half_of(half)],
        lambda half: src.at[(core,) + half_of(half)],
        sibling=True,
    )


def around(axes, sibling=True):
    partners = []
    for axis in axes:
        unused, right, unused, left = ring(axis)
        partners += [{axis: right}, {axis: left}]
    return partners + ([{"core": 1 - lax.axis_index("core")}] if sibling else [])


def load_columns(weight, own, width, at, loads, first):
    begin = pl.multiple_of(lax.axis_index("x") * width, 128)
    rows = own.shape[1]
    copies = [
        pltpu.make_async_copy(
            weight.at[pl.ds(c * rows, rows), pl.ds(begin, width)],
            own.at[c, :, pl.ds(at, width)],
            loads.at[first + c],
        )
        for c in range(2)
    ]
    for copy in copies:
        copy.start()
    return copies


def start_kernel(
    hidden, query, key, value, gains, hidden_out, qkv_out, gains_out, qkv, sends, recvs, loads
):
    me_x, me_y = lax.axis_index("x"), lax.axis_index("dp")
    far_y = lax.rem(me_y + 2, 4)
    slices = (
        load_columns(query, qkv, 256, 0, loads, 3)
        + load_columns(key, qkv, 128, 256, loads, 5)
        + load_columns(value, qkv, 128, 384, loads, 7)
    )
    own = [
        pltpu.make_async_copy(hidden, hidden_out.at[:, me_x], loads.at[0]),
        pltpu.make_async_copy(gains, gains_out.at[me_y], loads.at[2]),
    ]
    for copy in own:
        copy.start()
    partners = around(["x", "dp"])
    meet(partners + [{"dp": far_y}])
    send = Sends(sends, recvs)
    line = line_ring(send, hidden, hidden_out)
    line.begin()
    for copy in slices:
        copy.wait()
    own.append(pltpu.make_async_copy(qkv, qkv_out.at[me_y], loads.at[1]))
    own[-1].start()
    weights = weight_gather(send, qkv, qkv_out, rows_half(64))
    weights.begin()
    direct = [
        send(gains, gains_out.at[me_y], partner) for partner in partners[2:4] + [{"dp": far_y}]
    ]
    line.middle()
    weights.middle()
    for step in ("near", "end", "finish"):
        for gather in (weights, line):
            getattr(gather, step)()
    for copy in direct:
        copy.wait_recv()
    for copy in own:
        copy.wait()
    send.finish()


def start_gather(kernel_id, hidden_rows, query, key, value, gains):
    hidden, qkv, gains = pl.pallas_call(
        start_kernel,
        out_shape=(
            jax.ShapeDtypeStruct((2, 4, BLK, 1024), BF16),
            jax.ShapeDtypeStruct((4, 2, 128, 512), BF16),
            jax.ShapeDtypeStruct((4, 16, 128), BF16),
        ),
        in_specs=[VMEM] + [ANY] * 3 + [VMEM],
        out_specs=(ANY,) * 3,
        scratch_shapes=[pltpu.VMEM((2, 128, 512), BF16), sems(21), sems(21), sems(9)],
        compiler_params=pltpu.CompilerParams(collective_id=kernel_id, has_side_effects=True),
    )(hidden_rows.reshape(2, BLK, 1024), query, key, value, gains)
    return hidden.reshape(ROWS, 1024), qkv.reshape(1024, 512), gains


def line_gather_kernel(src, out, sends, recvs, loads):
    own = pltpu.make_async_copy(src, out.at[:, lax.axis_index("x")], loads.at[0])
    own.start()
    meet(around(["x"], sibling=False))
    send = Sends(sends, recvs)
    line = line_ring(send, src, out)
    for step in ("begin", "middle", "near", "end"):
        getattr(line, step)()
    own.wait()
    send.finish()


def line_ring(send, src, out):
    return RingGather(
        send, "x", lambda place, core, half: out.at[half, place], lambda half: src.at[half]
    )


def line_gather(kernel_id, rows):
    width = rows.shape[1]
    return pl.pallas_call(
        line_gather_kernel,
        out_shape=jax.ShapeDtypeStruct((2, 4, BLK, width), BF16),
        in_specs=[VMEM],
        out_specs=ANY,
        scratch_shapes=[sems(6), sems(6), sems(1)],
        compiler_params=pltpu.CompilerParams(collective_id=kernel_id, has_side_effects=True),
    )(rows.reshape(2, BLK, width)).reshape(ROWS, width)


def line_gather_pack_kernel(
    src, gate, up, down, out, packed_y, packed_z,
    gu_own, gu_sib, down_own, down_sib, sends, recvs, loads,
):
    core = lax.axis_index("core")
    to_sib = {"core": 1 - core}
    views = [
        (lambda c: gate.at[:, :, c], gu_own.at[0], gu_sib.at[0]),
        (lambda c: up.at[:, :, c], gu_own.at[1], gu_sib.at[1]),
        (lambda c: down.at[:, c], down_own, down_sib),
    ]
    local = [
        pltpu.make_async_copy(view(core), mine, loads.at[i])
        for i, (view, mine, unused) in enumerate(views)
    ]
    local.append(pltpu.make_async_copy(src, out.at[:, lax.axis_index("x")], loads.at[3]))
    for copy in local:
        copy.start()
    meet(around(["x"]))
    send = Sends(sends, recvs)
    line = line_ring(send, src, out)
    line.begin()
    shared = [send(view(1 - core), theirs, to_sib) for view, unused, theirs in views]
    line.middle()
    for copy in local:
        copy.wait()
    for copy in shared:
        copy.wait_recv()

    def pack(y, unused):
        for z in range(4):
            for s in range(2):

                def put(rows, value):
                    if s == 0:
                        packed_y[y, z, rows, :] = value
                    else:
                        packed_z[z, y, rows, :] = value

                for t in range(9):
                    cols = slice(t * 128, (t + 1) * 128)
                    put(
                        slice(t * 32, (t + 1) * 32),
                        add_low(gu_own[s, y, z, :, cols], gu_sib[s, y, z, :, cols]),
                    )
                cols = slice(s * 512 + z * 128, s * 512 + (z + 1) * 128)
                put(slice(288, 432), add_low(down_own[y, :, cols], down_sib[y, :, cols]))
        return unused

    lax.fori_loop(0, 4, pack, 0)
    line.near()
    line.end()
    send.finish()


def line_gather_pack(kernel_id, rows, gate, up, down):
    def vm(*shape):
        return pltpu.VMEM(shape, BF16)

    gathered, packed_y, packed_z = pl.pallas_call(
        line_gather_pack_kernel,
        out_shape=(jax.ShapeDtypeStruct((2, 4, BLK, 1024), BF16),)
        + (jax.ShapeDtypeStruct((4, 4, FF_PIECE, 128), BF16),) * 2,
        in_specs=[VMEM] + [ANY] * 3,
        out_specs=(ANY, VMEM, VMEM),
        scratch_shapes=[
            vm(2, 4, 4, 32, 1152), vm(2, 4, 4, 32, 1152),
            vm(4, 144, 1024), vm(4, 144, 1024),
            sems(9), sems(9), sems(4),
        ],
        compiler_params=pltpu.CompilerParams(
            collective_id=kernel_id, has_side_effects=True, vmem_limit_bytes=40 * 2**20
        ),
    )(
        rows.reshape(2, BLK, 1024),
        gate.reshape(4, 4, 2, 32, 1152),
        up.reshape(4, 4, 2, 32, 1152),
        down.reshape(4, 2, 144, 1024),
    )
    return gathered.reshape(ROWS, 1024), packed_y, packed_z


def sequence_gather_kernel(
    kv, gate, out, kv_all, gate_all, out_all, sends, recvs, loads
):
    me_z, me_y = lax.axis_index("z"), lax.axis_index("dp")
    core = lax.axis_index("core")
    own = [
        pltpu.make_async_copy(kv, kv_all.at[me_z, core], loads.at[0]),
        pltpu.make_async_copy(out, out_all.at[me_y], loads.at[2]),
        pltpu.make_async_copy(gate, gate_all.at[me_y], loads.at[1]),
    ]
    for copy in own:
        copy.start()
    meet(around(["z", "dp"]))
    send = Sends(sends, recvs)
    gathers = [
        RingGather(
            send,
            "z",
            lambda place, core, half: kv_all.at[place, core, half],
            lambda half: kv.at[half],
            sibling=True,
            share_own=True,
        ),
        weight_gather(send, out, out_all, columns_half(512)),
        weight_gather(send, gate, gate_all, rows_half(64)),
    ]
    gathers[0].begin()
    gathers[2].begin()
    gathers[1].begin()
    for step in ("middle", "near", "end", "finish"):
        for gather in gathers:
            getattr(gather, step)()
    for copy in own:
        copy.wait()
    send.finish()


def sequence_gather(kernel_id, kv, gate, out):
    kv_all, gate_all, out_all = pl.pallas_call(
        sequence_gather_kernel,
        out_shape=(
            jax.ShapeDtypeStruct((4, 2, 2, 2 * HD, ROWS), BF16),
            jax.ShapeDtypeStruct((4, 2, 128, 1152), BF16),
            jax.ShapeDtypeStruct((4, 2, 32, 1024), BF16),
        ),
        in_specs=[VMEM] * 3,
        out_specs=(ANY,) * 3,
        scratch_shapes=[sems(38), sems(38), sems(3)],
        compiler_params=pltpu.CompilerParams(collective_id=kernel_id, has_side_effects=True),
    )(kv, gate.reshape(2, 128, 1152), out.reshape(2, 32, 1024))
    return (
        kv_all.reshape(GROUPS, 2, 2 * HD, ROWS),
        gate_all.reshape(1024, 1152),
        out_all.reshape(256, 1024),
    )


def attend_kernel(
    q_ref, kv_ref, qo_ref, ko_ref, up, mixed_ref, low_ref, log_ref, up_all,
    sends, recvs, loads,
):
    meet(around(["dp"]))
    own = pltpu.make_async_copy(up, up_all.at[lax.axis_index("dp")], loads.at[0])
    own.start()
    send = Sends(sends, recvs)
    gather = weight_gather(send, up, up_all, rows_half(64))
    gather.begin()
    for half in range(2):
        cols = slice(half * HALF, (half + 1) * HALF)
        q_order = jnp.concatenate([qo_ref[:, cols]] * 2, axis=1)
        queries = [head_pair(q_ref, kv_head, cols) for kv_head in range(2)]

        def group(g, carried):
            carried = list(carried)
            for k_half in range(half + 1):
                keys = slice(k_half * HALF, (k_half + 1) * HALF)
                for kv_head in range(2):
                    acc, total = carried[kv_head]
                    probs = jnp.exp2(
                        scores_of(kv_ref[g, kv_head, 0:HD, keys], queries[kv_head]) * EXP2_SCALE
                    )
                    if k_half == half:
                        allowed = jnp.concatenate([ko_ref[g, keys, :]] * 4, axis=1) <= q_order
                        probs = jnp.where(allowed, probs, 0.0)
                    total = total + jnp.sum(probs, axis=0, keepdims=True)
                    acc = acc + dot(kv_ref[g, kv_head, HD : 2 * HD, keys], probs.astype(BF16))
                    carried[kv_head] = (acc, total)
            return tuple(carried)

        start = (jnp.zeros((HD, 2 * HALF), F32), jnp.zeros((1, 2 * HALF), F32))
        sums = lax.fori_loop(0, GROUPS, group, (start, start))
        for kv_head, (acc, total) in enumerate(sums):
            mixed = acc / total
            logs = jnp.log2(total)
            for head in range(2):
                at = 2 * kv_head + head
                rows = slice(at * HD, (at + 1) * HD)
                part = mixed[:, head * HALF : (head + 1) * HALF]
                mixed_ref[rows, cols] = part
                low_ref[rows, cols] = part.astype(BF16)
                log_ref[at : at + 1, cols] = logs[:, head * HALF : (head + 1) * HALF]
        if half == 0:
            gather.middle()
    gather.near()
    gather.end()
    gather.finish()
    own.wait()
    send.finish()


def attend(kernel_id, q_t, kv_all, q_order, k_order, up):
    *results, up_all = pl.pallas_call(
        attend_kernel,
        out_shape=(
            jax.ShapeDtypeStruct((4 * HD, ROWS), F32),
            jax.ShapeDtypeStruct((4 * HD, ROWS), BF16),
            jax.ShapeDtypeStruct((4, ROWS), F32),
            jax.ShapeDtypeStruct((4, 2, 128, 1152), BF16),
        ),
        in_specs=[VMEM] * 5,
        out_specs=(VMEM,) * 3 + (ANY,),
        scratch_shapes=[sems(12), sems(12), sems(1)],
        compiler_params=pltpu.CompilerParams(
            collective_id=kernel_id, has_side_effects=True, vmem_limit_bytes=40 * 2**20
        ),
    )(q_t, kv_all, q_order, k_order, up.reshape(2, 128, 1152))
    return *results, up_all.reshape(1024, 1152)


def add_low(left, right):
    return (left.astype(F32) + right.astype(F32)).astype(BF16)


def others(axis):
    return [{axis: place} for place in ring(axis)[1:]]


def send_to_others(send, axis, source, slots):
    slot = slots.at[lax.axis_index(axis)]
    return [send(source, slot, other) for other in others(axis)]


def send_each(send, axis, sources, slots):
    slot = slots.at[lax.axis_index(axis)]
    return [send(sources.at[place], slot, {axis: place}) for place in ring(axis)[1:]]


class LineSum:
    def __init__(self, part, buffers, loads, first):
        self.part = part
        self.pair, self.self_rows, self.far_in, self.left_in, self.right_in = buffers
        self.me, self.right, self.far, self.left = ring("x")
        self.to_right, self.to_left = {"x": self.right}, {"x": self.left}
        self.local = [
            pltpu.make_async_copy(part.at[0, self.right], self.pair.at[0], loads.at[first]),
            pltpu.make_async_copy(part.at[1, self.left], self.pair.at[1], loads.at[first + 1]),
            pltpu.make_async_copy(part.at[0, self.me], self.self_rows.at[0], loads.at[first + 2]),
            pltpu.make_async_copy(part.at[1, self.me], self.self_rows.at[1], loads.at[first + 3]),
        ]
        for copy in self.local:
            copy.start()

    def begin(self, send):
        part = self.part
        self.far0 = send(part.at[0, self.far], self.far_in.at[0], self.to_right)
        self.far1 = send(part.at[1, self.far], self.far_in.at[1], self.to_left)
        self.right1 = send(part.at[1, self.right], self.left_in.at[1], self.to_right)
        self.left0 = send(part.at[0, self.left], self.right_in.at[0], self.to_left)

    def middle(self, send):
        pair, far_in = self.pair, self.far_in
        self.local[0].wait()
        self.far0.wait_recv()
        pair[0] = add_low(pair[0], far_in[0])
        self.right0 = send(pair.at[0], self.left_in.at[0], self.to_right)
        self.local[1].wait()
        self.far1.wait_recv()
        pair[1] = add_low(pair[1], far_in[1])
        self.left1 = send(pair.at[1], self.right_in.at[1], self.to_left)

    def end(self, out):
        for copy in self.local[2:]:
            copy.wait()
        self.right1.wait_recv()
        self.left0.wait_recv()
        self.right0.wait_recv()
        self.left1.wait_recv()
        for h in range(2):
            out[h] = (
                self.self_rows[h].astype(F32)
                + self.left_in[h].astype(F32)
                + self.right_in[h].astype(F32)
            )


def line_buffers(width):
    return [pltpu.VMEM((2, BLK, width), BF16)] * 5


def line_scatter_kernel(rider, *refs):
    inputs, outputs = {None: (1, 1), "down": (2, 2), "pieces": (3, 3)}[rider]
    part, *riding = refs[:inputs]
    out, *riding_out = refs[inputs : inputs + outputs]
    *buffers, sends, recvs, loads = refs[inputs + outputs :]
    line = LineSum(part, buffers, loads, 0)
    own = []
    for i, (source, target) in enumerate(zip(riding, riding_out)):
        place = lax.axis_index("dp" if rider == "down" else ("z", "x")[i])
        own.append(pltpu.make_async_copy(source, target.at[place], loads.at[4 + i]))
        own[-1].start()
    if rider == "down":
        meet(around(["x", "dp"]))
    elif rider == "pieces":
        meet(others("z") + others("x"))
    else:
        meet(around(["x"], sibling=False))
    send = Sends(sends, recvs)
    line.begin(send)
    rings = []
    if rider == "down":
        rings = [weight_gather(send, riding[0], riding_out[0], columns_half(512))]
    direct = send_to_others(send, "z", *riding[:1], riding_out[0]) if rider == "pieces" else []
    for gather in rings:
        gather.begin()
    line.middle(send)
    if rider == "pieces":
        direct += send_to_others(send, "x", riding[1], riding_out[1])
    for gather in rings:
        gather.middle()
    for gather in rings:
        gather.near()
    line.end(out)
    for copy in own:
        copy.wait()
    for gather in rings:
        gather.end()
    for gather in rings:
        gather.finish()
    for copy in direct:
        copy.wait_recv()
    send.finish()


def line_scatter(kernel_id, partial, rider=None, riding=()):
    width = partial.shape[1]
    count = {None: 6, "down": 18, "pieces": 12}[rider]
    gathered = {None: (), "down": ((4, 2, 144, 1024),), "pieces": ((4, FF_PIECE, 128),) * 2}
    result = pl.pallas_call(
        functools.partial(line_scatter_kernel, rider),
        out_shape=(jax.ShapeDtypeStruct((2, BLK, width), F32),)
        + tuple(jax.ShapeDtypeStruct(shape, BF16) for shape in gathered[rider]),
        in_specs=[ANY] + [VMEM] * len(riding),
        out_specs=(VMEM,) + (ANY,) * len(riding),
        scratch_shapes=line_buffers(width) + [sems(count), sems(count), sems(6)],
        compiler_params=pltpu.CompilerParams(
            collective_id=kernel_id, has_side_effects=True, vmem_limit_bytes=32 * 2**20
        ),
    )(partial.reshape(2, 4, BLK, width), *riding)
    summed = result[0].reshape(2 * BLK, width)
    return (summed, *result[1:]) if rider else summed


class RingSum:
    def __init__(self, send, axis, chunk, far_in, left_in, right_in):
        self.send, self.chunk = send, chunk
        self.far_in, self.left_in, self.right_in = far_in, left_in, right_in
        self.me, self.right, self.far, self.left = ring(axis)
        self.to_right, self.to_left = {axis: self.right}, {axis: self.left}

    def begin(self):
        send, chunk = self.send, self.chunk
        self.far0 = send(chunk(self.far, 0), self.far_in(0), self.to_right)
        self.far1 = send(chunk(self.far, 1), self.far_in(1), self.to_left)
        self.right1 = send(chunk(self.right, 1), self.left_in(1), self.to_right)
        self.left0 = send(chunk(self.left, 0), self.right_in(0), self.to_left)

    def middle(self):
        send, chunk = self.send, self.chunk
        self.far0.wait_recv()
        mine = chunk(self.right, 0)
        mine[...] = add_low(mine[...], self.far_in(0)[...])
        self.right0 = send(mine, self.left_in(0), self.to_right)
        self.far1.wait_recv()
        mine = chunk(self.left, 1)
        mine[...] = add_low(mine[...], self.far_in(1)[...])
        self.left1 = send(mine, self.right_in(1), self.to_left)

    def end(self, store):
        self.right1.wait_recv()
        self.left0.wait_recv()
        self.right0.wait_recv()
        self.left1.wait_recv()
        for h in range(2):
            store(
                h,
                self.chunk(self.me, h)[...].astype(F32)
                + self.left_in(h)[...].astype(F32)
                + self.right_in(h)[...].astype(F32),
            )


def attend_back_kernel(
    q_ref, kv_ref, qo_ref, ko_ref, mixed_ref, log_ref, grad_ref, packed_y, packed_z,
    dq_ref, dkv_ref, mid_ref,
    dkv_acc, packed, far_in, left_in, right_in, sends, recvs, loads,
):
    local = [
        pltpu.make_async_copy(source, packed.at[i], loads.at[i])
        for i, source in enumerate((packed_y, packed_z))
    ]
    for copy in local:
        copy.start()
    meet(around(["dp", "z"], sibling=False))
    for copy in local:
        copy.wait()
    send = Sends(sends, recvs)
    two = (pl.ds(0, 2), pl.ds(2, 2))
    sums = [
        RingSum(
            send,
            axis,
            lambda place, h, s=s: packed.at[s, place, two[h]],
            lambda h, s=s: far_in.at[s, h],
            lambda h, s=s: left_in.at[s, h],
            lambda h, s=s: right_in.at[s, h],
        )
        for s, axis in enumerate(("dp", "z"))
    ]
    for step in sums:
        step.begin()

    dkv_acc[...] = jnp.zeros_like(dkv_acc)
    for half in range(2):
        cols = slice(half * HALF, (half + 1) * HALF)
        q_order = jnp.concatenate([qo_ref[:, cols]] * 2, axis=1)
        queries = [head_pair(q_ref, kv_head, cols) for kv_head in range(2)]
        grads = [head_pair(grad_ref, kv_head, cols) for kv_head in range(2)]
        logs = [
            jnp.concatenate([log_ref[at : at + 1, cols], log_ref[at + 1 : at + 2, cols]], axis=1)
            for at in (0, 2)
        ]
        dots = [
            jnp.sum(
                head_pair(mixed_ref, kv_head, cols) * grads[kv_head].astype(F32),
                axis=0,
                keepdims=True,
            )
            for kv_head in range(2)
        ]

        def group(g, carried):
            carried = list(carried)
            for k_half in range(half + 1):
                keys = slice(k_half * HALF, (k_half + 1) * HALF)
                for kv_head in range(2):
                    q_t, grad_t = queries[kv_head], grads[kv_head]
                    k_t = kv_ref[g, kv_head, 0:HD, keys]
                    v_t = kv_ref[g, kv_head, HD : 2 * HD, keys]
                    probs = jnp.exp2(scores_of(k_t, q_t) * EXP2_SCALE - logs[kv_head])
                    if k_half == half:
                        allowed = jnp.concatenate([ko_ref[g, keys, :]] * 4, axis=1) <= q_order
                        probs = jnp.where(allowed, probs, 0.0)
                    score_grad = (probs * (scores_of(v_t, grad_t) - dots[kv_head])).astype(BF16)
                    dkv_acc[g, kv_head, HD : 2 * HD, keys] += dot(
                        grad_t, probs.astype(BF16), 1, 1
                    )
                    dkv_acc[g, kv_head, 0:HD, keys] += dot(q_t, score_grad, 1, 1)
                    carried[kv_head] = carried[kv_head] + dot(k_t, score_grad)
            return tuple(carried)

        start = jnp.zeros((HD, 2 * HALF), F32)
        if half == 0:
            query_grads = lax.fori_loop(0, GROUPS, group, (start, start))
            for step in sums:
                step.middle()
        else:
            query_grads = lax.fori_loop(0, GROUPS, group, (start, start))
        for kv_head, dq in enumerate(query_grads):
            for head in range(2):
                at = 2 * kv_head + head
                rows = slice(at * HD, (at + 1) * HD)
                dq_ref[rows, cols] = dq[:, head * HALF : (head + 1) * HALF] * SCORE_SCALE

    def finish(g, unused):
        for kv_head in range(2):
            dkv_ref[g, kv_head, 0:HD, :] = (dkv_acc[g, kv_head, 0:HD, :] * SCORE_SCALE).astype(
                BF16
            )
            dkv_ref[g, kv_head, HD : 2 * HD, :] = dkv_acc[g, kv_head, HD : 2 * HD, :].astype(BF16)
        return unused

    lax.fori_loop(0, GROUPS, finish, 0)
    for s in range(2):

        def keep(half, value, s=s):
            mid_ref[s, 2 * half : 2 * half + 2] = value.astype(BF16)

        sums[s].end(keep)
    send.finish()


def attend_back(kernel_id, q_t, kv_all, q_order, k_order, mixed, log_total, mixed_grad, packed):
    return pl.pallas_call(
        attend_back_kernel,
        out_shape=(
            jax.ShapeDtypeStruct((4 * HD, ROWS), F32),
            jax.ShapeDtypeStruct((GROUPS, 2, 2 * HD, ROWS), BF16),
            jax.ShapeDtypeStruct((2, 4, FF_PIECE, 128), BF16),
        ),
        in_specs=[VMEM] * 7 + [ANY] * 2,
        out_specs=(VMEM,) * 3,
        scratch_shapes=[pltpu.VMEM((GROUPS, 2, 2 * HD, ROWS), F32)]
        + [pltpu.VMEM((2, 4, 4, FF_PIECE, 128), BF16)]
        + [pltpu.VMEM((2, 2, 2, FF_PIECE, 128), BF16)] * 3
        + [sems(12), sems(12), sems(2)],
        compiler_params=pltpu.CompilerParams(
            collective_id=kernel_id, has_side_effects=True, vmem_limit_bytes=48 * 2**20
        ),
    )(q_t, kv_all, q_order, k_order, mixed, log_total, mixed_grad, *packed)


def sequence_scatter_kernel(
    part, mid, line_part, out, piece, line_out,
    own, other, far_in, left_in, right_in, slots, pair, self_rows, line_far, line_left, line_right,
    sends, recvs, loads,
):
    core = lax.axis_index("core")
    me, right, far, left = ring("z")
    order = (far, right, left, me)
    local = [
        pltpu.make_async_copy(part.at[place, core], own.at[place], loads.at[i])
        for i, place in enumerate(order)
    ]
    for copy in local:
        copy.start()
    line = LineSum(line_part, (pair, self_rows, line_far, line_left, line_right), loads, 4)
    to_sib = {"core": 1 - core}
    meet(others("z") + others("dp") + around(["x"], sibling=False) + [to_sib])
    send = Sends(sends, recvs)
    shared = [send(part.at[place, 1 - core], other.at[place], to_sib) for place in order]

    def merge(i):
        local[i].wait()
        shared[i].wait_recv()
        own[order[i]] = add_low(own[order[i]], other[order[i]])

    ring_sum = RingSum(
        send,
        "z",
        lambda place, h: own.at[place, h],
        lambda h: far_in.at[h],
        lambda h: left_in.at[h],
        lambda h: right_in.at[h],
    )
    for i in range(3):
        merge(i)
    ring_sum.begin()
    line.begin(send)
    direct = send_each(send, "dp", mid.at[1], slots.at[1])
    merge(3)
    ring_sum.middle()
    direct += send_each(send, "z", mid.at[0], slots.at[0])
    line.middle(send)

    def store(h, value):
        out[h] = value

    ring_sum.end(store)
    line.end(line_out)
    for copy in direct:
        copy.wait_recv()
    for s, axis in enumerate(("z", "dp")):
        me, *places = ring(axis)
        total = mid[s, me].astype(F32)
        for place in places:
            total = total + slots[s, place].astype(F32)
        piece[s] = total.astype(BF16)
    send.finish()


def sequence_scatter(kernel_id, partial, mid, line_part):
    buffer = pltpu.VMEM((2, 2 * HD, ROWS), BF16)
    wide = pltpu.VMEM((4, 2, 2 * HD, ROWS), BF16)
    return pl.pallas_call(
        sequence_scatter_kernel,
        out_shape=(
            jax.ShapeDtypeStruct((2, 2 * HD, ROWS), F32),
            jax.ShapeDtypeStruct((2, FF_PIECE, 128), BF16),
            jax.ShapeDtypeStruct((2, BLK, 1024), F32),
        ),
        in_specs=[ANY, VMEM, ANY],
        out_specs=(VMEM,) * 3,
        scratch_shapes=[wide, wide, buffer, buffer, buffer]
        + [pltpu.VMEM((2, 4, FF_PIECE, 128), BF16)]
        + line_buffers(1024)
        + [sems(22), sems(22), sems(8)],
        compiler_params=pltpu.CompilerParams(
            collective_id=kernel_id, has_side_effects=True, vmem_limit_bytes=32 * 2**20
        ),
    )(partial.reshape(4, 2, 2, 2 * HD, ROWS), mid, line_part)


def tail_kernel(
    qkv, out, gains, ff_a, ff_b, gain_sums, ff_out, qkv_out, out_out,
    qkv_own, qkv_sib, out_own, out_sib, gain_slots,
    packed, slots_y, mid, slots_z, qkv_line, out_x, out_y,
    sends, recvs, loads,
):
    core = lax.axis_index("core")
    me_x, me_y, me_z = lax.axis_index("x"), lax.axis_index("dp"), lax.axis_index("z")
    to_sib = {"core": 1 - core}
    views = [
        (lambda c: qkv.at[:, :, c], qkv_own, qkv_sib),
        (lambda c: out.at[:, c], out_own, out_sib),
    ]
    local = [
        pltpu.make_async_copy(view(core), mine, loads.at[i])
        for i, (view, mine, unused) in enumerate(views)
    ]
    own = [
        pltpu.make_async_copy(ff_a, ff_out.at[0, core, :, me_x], loads.at[2]),
        pltpu.make_async_copy(ff_b, ff_out.at[1, core, me_z], loads.at[3]),
    ]
    for copy in local + own:
        copy.start()
    meet(others("z") + others("dp") + others("x") + [to_sib])
    send = Sends(sends, recvs)

    def arrived(copies):
        for copy in copies:
            copy.wait_recv()

    def gain_begin(step, axis, value):
        place = lax.axis_index(axis)
        gain_slots[step, place] = value
        slot = gain_slots.at[step, place]
        return [send(slot, slot, to) for to in ([to_sib] if axis == "core" else others(axis))]

    def gain_end(step, copies):
        arrived(copies)
        total = gain_slots[step, 0] + gain_slots[step, 1]
        for place in range(2, 4 if step else 2):
            total = total + gain_slots[step, place]
        return total

    gain_copies = gain_begin(0, "core", gains[...])
    shared = [send(view(1 - core), theirs, to_sib) for view, unused, theirs in views]
    two = (pl.ds(0, 2), pl.ds(2, 2))
    bulk = [
        RingGather(
            send,
            "x",
            lambda place, core, half: ff_out.at[0, core, two[half], place],
            lambda half: ff_a.at[two[half]],
            sibling=True,
            share_own=True,
        ),
        RingGather(
            send,
            "z",
            lambda place, core, half: ff_out.at[1, core, place, two[half]],
            lambda half: ff_b.at[two[half]],
            sibling=True,
            share_own=True,
        ),
    ]
    for gather in bulk:
        gather.begin()
    for copy in local:
        copy.wait()
    arrived(shared)

    def pack(y, unused):
        for z in range(4):
            for t in range(4):
                cols = slice(t * 128, (t + 1) * 128)
                packed[y, z, t * 32 : (t + 1) * 32, :] = add_low(
                    qkv_own[y, z, :, cols], qkv_sib[y, z, :, cols]
                )
            for s in range(2):
                cols = slice(s * 512 + z * 128, s * 512 + (z + 1) * 128)
                packed[y, z, 128 + s * 32 : 160 + s * 32, :] = add_low(
                    out_own[y, :, cols], out_sib[y, :, cols]
                )
        return unused

    lax.fori_loop(0, 4, pack, 0)
    to_y = send_each(send, "dp", packed, slots_y)
    gain_copies = gain_begin(1, "z", gain_end(0, gain_copies))
    for gather in bulk:
        gather.middle()
    gain_copies = gain_begin(2, "dp", gain_end(1, gain_copies))
    arrived(to_y)
    total = packed[me_y].astype(F32)
    for place in ring("dp")[1:]:
        total = total + slots_y[place].astype(F32)
    mid[...] = total.astype(BF16)
    to_z = send_each(send, "z", mid, slots_z)
    gain_copies = gain_begin(3, "x", gain_end(2, gain_copies))
    arrived(to_z)
    total = mid[me_z].astype(F32)
    for place in ring("z")[1:]:
        total = total + slots_z[place].astype(F32)
    total = total.astype(BF16)
    qkv_line[me_z] = total[0:128]
    out_x[me_x] = total[128:192]
    qkv_z = send_to_others(send, "z", qkv_line.at[me_z], qkv_line)
    out_line = send_to_others(send, "x", out_x.at[me_x], out_x)
    for gather in bulk:
        gather.near()
    arrived(out_line)
    out_y[me_y] = out_x[me_y]
    out_places = send_each(send, "dp", out_x, out_y)
    arrived(qkv_z)
    own.append(pltpu.make_async_copy(qkv_line, qkv_out.at[core, me_x], loads.at[4]))
    own[-1].start()
    qkv_x = send_to_others(send, "x", qkv_line, qkv_out.at[core])
    for gather in bulk:
        gather.end()
    arrived(out_places)
    own.append(pltpu.make_async_copy(out_y, out_out.at[core, me_z], loads.at[5]))
    own[-1].start()
    out_z = send_to_others(send, "z", out_y, out_out.at[core])
    gain_sums[...] = gain_end(3, gain_copies)
    for copy in own:
        copy.wait()
    arrived(qkv_x)
    last = [send(qkv_out.at[core], qkv_out.at[core], to_sib)]
    arrived(out_z)
    last.append(send(out_out.at[core], out_out.at[core], to_sib))
    for gather in bulk:
        gather.finish()
    arrived(last)
    send.finish()


def tail(kernel_id, qkv, out, gains, ff_a, ff_b):
    def vm(*shape):
        return pltpu.VMEM(shape, BF16)

    return pl.pallas_call(
        tail_kernel,
        out_shape=(
            jax.ShapeDtypeStruct((24, 128), F32),
            jax.ShapeDtypeStruct((2, 2, 4, 4, FF_PIECE, 128), BF16),
            jax.ShapeDtypeStruct((2, 4, 4, 128, 128), BF16),
            jax.ShapeDtypeStruct((2, 4, 4, 64, 128), BF16),
        ),
        in_specs=[ANY] * 2 + [VMEM] * 3,
        out_specs=(VMEM, ANY, ANY, ANY),
        scratch_shapes=[
            vm(4, 4, 32, 512), vm(4, 4, 32, 512),
            vm(4, 32, 1024), vm(4, 32, 1024),
            pltpu.VMEM((4, 4, 24, 128), F32),
            vm(4, 4, 192, 128), vm(4, 4, 192, 128),
            vm(4, 192, 128), vm(4, 192, 128),
            vm(4, 128, 128), vm(4, 64, 128), vm(4, 64, 128),
            sems(64), sems(64), sems(6),
        ],
        compiler_params=pltpu.CompilerParams(
            collective_id=kernel_id, has_side_effects=True, vmem_limit_bytes=48 * 2**20
        ),
    )(qkv.reshape(4, 4, 2, 32, 512), out.reshape(4, 2, 32, 1024), gains, ff_a, ff_b)


def unpack_rows_kernel(ff_pieces, qkv, gate, up, query, key, value):
    for x in range(4):
        for s, target in enumerate((gate, up)):
            row = jnp.concatenate(
                [
                    ff_pieces[s, 0, 0, x, t * 32 : (t + 1) * 32, :].astype(F32)
                    for t in range(9)
                ],
                axis=1,
            )
            for part in range(4):
                begin = part * 1152 + x * 288
                target[:, begin : begin + 288] = row[:, part * 288 : (part + 1) * 288]
        for t in range(2):
            cols = slice(x * 256 + t * 128, x * 256 + (t + 1) * 128)
            query[:, cols] = qkv[0, x, 0, t * 32 : (t + 1) * 32, :].astype(F32)
        cols = slice(x * 128, (x + 1) * 128)
        key[:, cols] = qkv[0, x, 0, 64:96, :].astype(F32)
        value[:, cols] = qkv[0, x, 0, 96:128, :].astype(F32)


def unpack_columns_kernel(ff_pieces, pieces, down, out):
    for s in range(2):
        for z in range(4):
            cols = slice(s * 512 + z * 128, s * 512 + (z + 1) * 128)
            down[:, cols] = ff_pieces[s, 0, z, 0].astype(F32)
            out[:, cols] = pieces[0, z, 0, s * 32 : (s + 1) * 32, :].astype(F32)


def unpack(ff_pieces, qkv, out):
    rows = pl.pallas_call(
        unpack_rows_kernel,
        grid=(4, 2),
        out_shape=tuple(
            jax.ShapeDtypeStruct((256, width), F32) for width in (4608, 4608, 1024, 512, 512)
        ),
        in_specs=[
            pl.BlockSpec((2, 1, 1, 4, 288, 128), lambda z, c: (0, c, z, 0, 0, 0)),
            pl.BlockSpec((1, 4, 1, 128, 128), lambda z, c: (c, 0, z, 0, 0)),
        ],
        out_specs=tuple(
            pl.BlockSpec((32, width), lambda z, c: (2 * z + c, 0))
            for width in (4608, 4608, 1024, 512, 512)
        ),
        compiler_params=pltpu.CompilerParams(vmem_limit_bytes=32 * 2**20),
    )(ff_pieces, qkv)
    columns = pl.pallas_call(
        unpack_columns_kernel,
        grid=(4, 2),
        out_shape=(
            jax.ShapeDtypeStruct((1152, 1024), F32),
            jax.ShapeDtypeStruct((256, 1024), F32),
        ),
        in_specs=[
            pl.BlockSpec((2, 1, 4, 1, 144, 128), lambda x, c: (0, c, 0, x, 2, 0)),
            pl.BlockSpec((1, 4, 1, 64, 128), lambda x, c: (c, 0, x, 0, 0)),
        ],
        out_specs=(
            pl.BlockSpec((144, 1024), lambda x, c: (2 * x + c, 0)),
            pl.BlockSpec((32, 1024), lambda x, c: (2 * x + c, 0)),
        ),
        compiler_params=pltpu.CompilerParams(vmem_limit_bytes=32 * 2**20),
    )(ff_pieces, out)
    return rows + columns


def after(value, anchor):
    return lax.optimization_barrier((value, anchor))[0]


def ff_columns_kernel(gate, up, gate_own, up_own):
    x_at = lax.axis_index("x")
    for x in range(4):

        @pl.when(x_at == x)
        def take(x=x):
            for source, target in ((gate, gate_own), (up, up_own)):
                for part in range(4):
                    begin = part * 1152 + x * 288
                    target[:, part * 288 : (part + 1) * 288] = (
                        source[:, begin : begin + 288].astype(F32).astype(BF16)
                    )


def ff_columns(gate, up):
    return pl.pallas_call(
        ff_columns_kernel,
        grid=(4,),
        out_shape=(jax.ShapeDtypeStruct((256, 1152), BF16),) * 2,
        in_specs=[pl.BlockSpec((64, 4608), lambda i: (i, 0))] * 2,
        out_specs=(pl.BlockSpec((64, 1152), lambda i: (i, 0)),) * 2,
        compiler_params=pltpu.CompilerParams(vmem_limit_bytes=32 * 2**20),
    )(gate, up)


SWAP = [(a * 4 + b, b * 4 + a) for a in range(4) for b in range(4)]


def on_device(
    hidden_in,
    positions,
    block_of,
    attn_gain,
    query_weight,
    key_weight,
    value_weight,
    out_weight,
    query_gain,
    key_gain,
    ffn_gain,
    gate_weight,
    up_weight,
    down_weight,
    cotangent,
):
    z_at = lax.axis_index("z")
    x_at = lax.axis_index("x")
    core_at = lax.axis_index("core")
    dp_at = lax.axis_index("dp")

    hidden_rows = hidden_in[0]
    grad_rows = cotangent[0]

    in_block = jnp.arange(BLK, dtype=jnp.int32)
    blocks = block_of.reshape(4, 4, 2, 2).transpose(0, 2, 3, 1)
    order_all = (blocks[..., None] * BLK + in_block).reshape(GROUPS, ROWS)
    own_order = lax.dynamic_index_in_dim(order_all, z_at * 2 + core_at, 0, keepdims=True)
    k_order = blocks.reshape(GROUPS, 8, 1, 1) * BLK + lax.broadcasted_iota(
        jnp.int32, (GROUPS, 8, BLK, 128), 2
    )
    k_order = k_order.reshape(GROUPS, ROWS, 128)
    own_slot = 2 * (z_at * 8 + x_at * 2 + core_at)
    first_block = lax.dynamic_index_in_dim(block_of, own_slot, 0, keepdims=False)
    offset = positions[0, 0] - first_block * BLK
    frequency = ROPE_BASE ** (-2.0 * jnp.arange(HD // 2, dtype=F32) / HD)
    angles = (own_order + offset).astype(F32) * frequency[:, None]
    cosine, sine = jnp.cos(angles), jnp.sin(angles)

    def swapped_rows(weight, rows):
        own = lax.dynamic_slice_in_dim(weight, x_at * rows, rows, axis=0)
        return lax.ppermute(own, ("dp", "x"), SWAP)

    gate_own, up_own = ff_columns(gate_weight, up_weight)
    down_own = lax.dynamic_slice_in_dim(down_weight, x_at * 288, 288, axis=0)
    gains_own = jnp.pad(
        jnp.concatenate([attn_gain, ffn_gain, query_gain, key_gain]), (0, 2048 - 544)
    )
    hidden = hidden_rows.astype(F32)
    line_hidden, qkv_weight, gains = start_gather(
        0, hidden_rows, query_weight, key_weight, value_weight, gains_own.reshape(16, 128)
    )
    gains = gains.reshape(4, 2048).astype(F32)
    attn_gain_all = gains[:, 0:256].reshape(1024)
    ffn_gain_all = gains[:, 256:512].reshape(1024)
    query_gain_all = gains[:, 512:528].reshape(HD)
    key_gain_all = gains[:, 528:544].reshape(HD)
    out_own = swapped_rows(after(out_weight, line_hidden), 64)
    branch_low = lax.all_gather(after(grad_rows, line_hidden).reshape(2, BLK, 1024), "x", axis=1).reshape(ROWS, 1024)
    attn_in = rms_scale(line_hidden.astype(F32), attn_gain_all).astype(BF16)
    qkv_t = dot(qkv_weight, attn_in, 0, 1)
    q_rot, q_back = jax.vjp(
        lambda r, g: head_norm_rope(r, g, cosine, sine),
        qkv_t[0:256].reshape(4, HD, ROWS),
        query_gain_all,
    )
    k_rot, k_back = jax.vjp(
        lambda r, g: head_norm_rope(r, g, cosine, sine),
        qkv_t[256:384].reshape(2, HD, ROWS),
        key_gain_all,
    )
    q_low = q_rot.reshape(4 * HD, ROWS).astype(BF16)
    kv_low = jnp.concatenate([k_rot, qkv_t[384:512].reshape(2, HD, ROWS)], axis=1).astype(BF16)
    kv_all, gate_slice, out_slice = sequence_gather(
        1, kv_low, gate_own, out_own
    )
    mixed, attn_low, log_total, up_slice = attend(
        10, q_low, kv_all, own_order, k_order, up_own
    )
    attn_rows, down_slice = line_scatter(
        2, dot(attn_low, out_slice, 0, 0).astype(BF16), "down", (down_own.reshape(2, 144, 1024),)
    )
    down_slice = down_slice.reshape(1152, 1024)
    after_attn = hidden + attn_rows
    normed_ffn, norm_ffn_back = jax.vjp(rms_scale, after_attn, ffn_gain_all)
    ffn_in = line_gather(3, normed_ffn.astype(BF16))
    gate_proj = dot(ffn_in, gate_slice)
    up_proj = dot(ffn_in, up_slice)
    activated, swiglu_back = jax.vjp(lambda g, u: jax.nn.silu(g) * u, gate_proj, up_proj)
    activated_low = activated.astype(BF16)
    residual_grad = grad_rows.astype(F32)
    activated_grad = dot(branch_low, down_slice, 1, 1)
    gate_grad, up_grad = swiglu_back(activated_grad)
    gate_grad_low = gate_grad.astype(BF16)
    up_grad_low = up_grad.astype(BF16)
    ffn_in_grad = line_scatter(
        5,
        (dot(gate_grad_low, gate_slice, 1, 1) + dot(up_grad_low, up_slice, 1, 1)).astype(BF16),
    )
    mid_part, ffn_gain_part = norm_ffn_back(ffn_in_grad)
    mid_grad = residual_grad + mid_part
    branch_attn, packed_y, packed_z = line_gather_pack(
        6,
        mid_grad.astype(BF16),
        dot(ffn_in, gate_grad_low, 0, 0).astype(BF16),
        dot(ffn_in, up_grad_low, 0, 0).astype(BF16),
        dot(activated_low, branch_low, 0, 0).astype(BF16),
    )
    out_part = dot(activated_low, down_slice).astype(BF16).reshape(2, 4, BLK, 1024)

    mixed_grad = dot(out_slice, branch_attn, 1, 1).astype(BF16)
    q_grad, kv_grad_all, ff_mid = attend_back(
        11, q_low, kv_all, own_order, k_order, mixed, log_total, mixed_grad, (packed_y, packed_z)
    )
    kv_grad, ff_piece, out_rows = sequence_scatter(7, kv_grad_all, ff_mid, out_part)
    layer_out = (after_attn + out_rows.reshape(2 * BLK, 1024)).astype(BF16)
    q_pre, q_gain_part = q_back(q_grad.reshape(4, HD, ROWS))
    k_pre, k_gain_part = k_back(kv_grad[:, 0:HD])
    qkv_pre = jnp.concatenate(
        [
            q_pre.reshape(4 * HD, ROWS),
            k_pre.reshape(2 * HD, ROWS),
            kv_grad[:, HD:].reshape(2 * HD, ROWS),
        ],
        axis=0,
    ).astype(BF16)
    attn_in_grad, ff_a, ff_b = line_scatter(
        8,
        dot(qkv_pre, qkv_weight, 0, 1).astype(BF16),
        "pieces",
        (ff_piece[0], ff_piece[1]),
    )
    unused, norm_attn_back = jax.vjp(rms_scale, hidden, attn_gain_all)
    hidden_part, attn_gain_part = norm_attn_back(attn_in_grad)
    input_grad = (mid_grad + hidden_part).astype(BF16)

    gain_parts = jnp.concatenate([attn_gain_part, ffn_gain_part, q_gain_part, k_gain_part])
    gain_parts = jnp.pad(gain_parts, (0, 3072 - 2176)).reshape(24, 128)

    def own_slice(begin, size):
        return lax.dynamic_slice_in_dim(
            gain_sums[begin : begin + size], dp_at * (size // 4), size // 4
        )

    gain_sums, ff_pieces, qkv_pieces, out_pieces = tail(
        9,
        dot(attn_in, qkv_pre, 0, 1).astype(BF16),
        dot(attn_low, branch_attn).astype(BF16),
        gain_parts,
        ff_a,
        ff_b,
    )
    gain_sums = gain_sums.reshape(3072)
    gate_all, up_all, query_all, key_all, value_all, down_all, out_all = unpack(
        ff_pieces, qkv_pieces, out_pieces
    )
    return (
        layer_out[None],
        input_grad[None],
        own_slice(0, 1024),
        query_all,
        key_all,
        value_all,
        out_all,
        own_slice(2048, 64),
        own_slice(2112, 64),
        own_slice(1024, 1024),
        gate_all,
        up_all,
        down_all,
    )


def solution(mesh):
    fine = Mesh(mesh.devices.reshape(4, 4, 4, 2), ("dp", "z", "x", "core"))
    ctx = ("z", "x", "core")
    rows = P("dp", ctx, None)
    vector, matrix = P("dp"), P("dp", None)
    return jax.shard_map(
        on_device,
        mesh=fine,
        in_specs=(rows, P("dp", ctx), P(), vector)
        + (matrix,) * 4
        + (vector,) * 3
        + (matrix,) * 3
        + (rows,),
        out_specs=(rows, rows, vector) + (matrix,) * 4 + (vector,) * 3 + (matrix,) * 3,
        check_vma=False,
    )
```
